32 devices in a mesh: parts: 2 (over x), lon: 16 (over z, y, core).
Axes of the slice: x: 2, y: 2, z: 4, core: 2. Of those that a mesh axis runs over, the one named last changes fastest.
Arguments:
- cotangent: float32 [96, 2048, 256], P(None, ('parts', 'lon')), parts along dimension 1, may hold values from -6 to 6
- synthesis: float32 [96, 96], replicated, may hold values from -0.625 to 0.625
- analysis: float32 [96, 96], replicated, may hold values from -0.625 to 0.625
- depths: float32 [96], replicated, may hold values from 0.2 to 5
- metric: float32 [1024, 256], P('lon'), may hold values from 0.5 to 2
- east_face: float32 [1024, 256], P('lon'), may hold values from 0.1 to 1
- north_face: float32 [1024, 256], P('lon'), may hold values from 0.1 to 1
Outputs:
- right_cotangent: float32 [96, 2048, 256], P(None, ('parts', 'lon')), parts along dimension 1
The draws below stay inside these ranges and needn't reach their ends.
There are 2 independent parts, one for each index of `parts`. The reference program is written for one: setup_inputs(seed, part) draws one part's arguments, and reference() takes and returns one part's arrays. A program takes and returns all parts, laid end to end along the dimension named above; an argument that names none is the same for every part. Nothing has to cross between parts.
All inputs are finite; a program needn't handle non-finite values.
Results may differ from the reference program's by a relative error of at most 0.000073.
Values sent between devices are 32-bit elements; how exact they have to be, the bound alone decides.
No kernel may reach another device: no remote copies, remote signals or barrier semaphores. Data moves between devices by JAX's collectives and lax.ppermute only.
A program may use at most 192 MiB of HBM per device.

```python
import math
import jax
import jax.numpy as jnp
from jax import lax

LEV = 96
NLAT = 256
ITERS = 4
NLON = 1024


def shard_levels(own_key, shape, shards, low, high):
    gain, own = 1.0, jax.random.fold_in(own_key, 6)
    for dim, parts in shards:
        draws = jnp.exp(jax.random.uniform(jax.random.fold_in(own, dim), (parts,), jnp.float32, low / len(shards), high / len(shards)))
        gain = gain * jnp.repeat(draws, shape[dim] // parts).reshape([-1 if axis == dim else 1 for axis in range(len(shape))])
    return gain


def noise(key, extent, spread, most, cuts=(), kind=jnp.bfloat16):
    entries = spread * jax.random.normal(key, extent, jnp.float32)
    if cuts:
        entries = entries * shard_levels(key, extent, cuts, -0.22, 0.18)
    return jnp.clip(entries, -most, most).astype(kind)


def setup_inputs(seed: int = 0, part: int = 0) -> dict:
    seeds = jax.random.split(jax.random.key(seed), 8)
    part_splits = jax.random.split(jax.random.fold_in(seeds[7], part), 8)
    return {
        "cotangent": noise(part_splits[0], (LEV, NLON, NLAT), 1.0, 6.0, ((1, 16),), jnp.float32),
        "synthesis": noise(seeds[1], (LEV, LEV), LEV ** -0.5, 0.625, (), jnp.float32),
        "analysis": noise(seeds[2], (LEV, LEV), LEV ** -0.5, 0.625, (), jnp.float32),
        "depths": jnp.clip(jnp.exp(jax.random.uniform(seeds[3], (LEV,), jnp.float32, math.log(0.2), math.log(5.0))), 0.2, 5.0),
        "metric": jnp.clip(0.5 + 1.5 * jax.random.uniform(seeds[4], (NLON, NLAT), jnp.float32) ** shard_levels(seeds[4], (NLON, NLAT), ((0, 16),), -0.2, 0.2), 0.5, 2.0),
        "east_face": jnp.clip(0.1 + 0.9 * jax.random.uniform(seeds[5], (NLON, NLAT), jnp.float32) ** shard_levels(seeds[5], (NLON, NLAT), ((0, 16),), -0.2, 0.2), 0.1, 1.0),
        "north_face": jnp.clip(0.1 + 0.9 * jax.random.uniform(seeds[6], (NLON, NLAT), jnp.float32) ** shard_levels(seeds[6], (NLON, NLAT), ((0, 16),), -0.2, 0.2), 0.1, 1.0),
    }


def apply_operator(field, eigen, coeffs):
    metric = coeffs[0]
    east_face = coeffs[1]
    north_face = coeffs[2]
    west_face = jnp.roll(east_face, 1, axis=0)
    south_face = jnp.concatenate([jnp.zeros_like(north_face[:, :1]), north_face[:, :-1]], axis=1)
    diagonal = eigen[:, None, None] * metric + east_face + west_face + north_face + south_face
    zero_row = jnp.zeros_like(field[:, :, :1])
    north_value = jnp.concatenate([field[:, :, 1:], zero_row], axis=2)
    south_value = jnp.concatenate([zero_row, field[:, :, :-1]], axis=2)
    return (diagonal * field - east_face * jnp.roll(field, -1, axis=1) - west_face * jnp.roll(field, 1, axis=1)
            - north_face * north_value - south_face * south_value)


def chebyshev(rhs, eigen, operator):
    lower_bound = 0.5 * eigen
    upper_bound = 2.0 * eigen + 8.0
    centre = ((upper_bound + lower_bound) / 2.0)[:, None, None]
    half_width = ((upper_bound - lower_bound) / 2.0)[:, None, None]
    sigma_ratio = centre / half_width
    rho_now = 1.0 / sigma_ratio
    update = rhs / centre
    solution = update
    residual = rhs
    for counter in range(ITERS):
        residual = residual - operator(update)
        rho_next = 1.0 / (2.0 * sigma_ratio - rho_now)
        update = rho_next * rho_now * update + (2.0 * rho_next / half_width) * residual
        solution = solution + update
        rho_now = rho_next
    return solution


def reference(cotangent, synthesis, analysis, depths, metric, east_face, north_face):
    levels, lon_count, lat_count = cotangent.shape
    modal = jnp.dot(synthesis.T, cotangent.reshape(levels, -1), precision=lax.Precision.HIGHEST,
                    preferred_element_type=jnp.float32).reshape(levels, lon_count, lat_count)
    coeffs = jnp.stack([metric, east_face, north_face])

    def operator(field):
        return apply_operator(field, depths, coeffs)

    solved = chebyshev(modal, depths, operator)
    return jnp.dot(analysis.T, solved.reshape(levels, -1), precision=lax.Precision.HIGHEST,
                   preferred_element_type=jnp.float32).reshape(levels, lon_count, lat_count)
```

```python
import functools
import math

import jax
import jax.numpy as jnp
from jax import lax
from jax.experimental import pallas as pl
from jax.experimental.pallas import tpu as pltpu
from jax.sharding import PartitionSpec as P

G = 16
H = 128
VMEM_LIMIT = 56 * 1024 * 1024
COS1, COS2 = math.cos(2 * math.pi / 5), math.cos(4 * math.pi / 5)
SIN1, SIN2 = math.sin(2 * math.pi / 5) ** 2, math.sin(4 * math.pi / 5) ** 2


def column(row):
    n = row.shape[1]
    eye = lax.broadcasted_iota(jnp.int32, (n, n), 0) == lax.broadcasted_iota(jnp.int32, (n, n), 1)
    picked = jnp.sum(jnp.where(eye, jnp.broadcast_to(row, (n, n)), 0.0), axis=1, keepdims=True)
    return jnp.broadcast_to(picked, (n, H))


def split(x):
    high = x.astype(jnp.bfloat16)
    low = (x - high.astype(jnp.float32)).astype(jnp.bfloat16)
    return high, low


def prepare(depths_ref, syn_ref, ana_ref, cols_ref, ws_ref, wa_ref):
    row = depths_ref[...]
    centre = 1.25 * row + 4.0
    half = 0.75 * row + 4.0
    product = row * (row + 4.0)
    c2, h2 = centre * centre, half * half
    gain = 16.0 / (centre * (16.0 * c2 * c2 - 20.0 * c2 * h2 + 5.0 * h2 * h2))
    d = column(row)
    cols_ref[0] = d
    cols_ref[1] = (1.0 - COS1) * (1.25 * d + 4.0)
    cols_ref[2] = (1.0 - COS2) * (1.25 * d + 4.0)
    cols_ref[3] = SIN1 * (d * (d + 4.0))
    cols_ref[4] = SIN2 * (d * (d + 4.0))
    n = row.shape[1]
    for src, dst, scale in ((syn_ref[...].T, ws_ref, None), (ana_ref[...].T, wa_ref, gain)):
        if scale is not None:
            src = src * scale
        high, low = split(src)
        dst[:, :n] = high
        dst[:, n : 2 * n] = high
        dst[:, 2 * n :] = low


def mix(weights, field):
    high, low = split(field)
    stacked = jnp.concatenate([high, low, high], axis=0)
    return jnp.dot(weights, stacked, preferred_element_type=jnp.float32)


def halves(ref, slot, rows):
    return ref[slot, rows, :H], ref[slot, rows, H:]


def put(ref, slot, rows, pair):
    ref[slot, rows, :H] = pair[0]
    ref[slot, rows, H:] = pair[1]


def coefficients(co_ref, k):
    e = co_ref[0, pl.ds(k, 1), :]
    w = co_ref[0, pl.ds(k - 1, 1), :]
    n = co_ref[1, pl.ds(k, 1), :]
    s = co_ref[2, pl.ds(k, 1), :]
    return tuple((c[:, :H], c[:, H:]) for c in (e, w, n, s))


def operate(diag, y, east, west, co):
    lanes = lax.broadcasted_iota(jnp.int32, (G, H), 1)
    (ea, eb), (wa, wb), (na, nb), (sa, sb) = co
    ya, yb = y
    na_r, nb_r = pltpu.roll(ya, H - 1, 1), pltpu.roll(yb, H - 1, 1)
    sa_r, sb_r = pltpu.roll(ya, 1, 1), pltpu.roll(yb, 1, 1)
    na_r = jnp.where(lanes == H - 1, nb_r, na_r)
    sb_r = jnp.where(lanes == 0, sa_r, sb_r)
    a = (diag[0] * ya - ea * east[0]) - (wa * west[0] + na * na_r + sa * sa_r)
    b = (diag[1] * yb - eb * east[1]) - (wb * west[1] + nb * nb_r + sb * sb_r)
    return a, b


def fill_coefficients(co_ref, at, metric, east, north):
    rows = metric.shape[0]
    lanes = lax.broadcasted_iota(jnp.int32, (rows, H), 1)
    na, nb = north[:, :H], north[:, H:]
    sa, sb = pltpu.roll(na, 1, 1), pltpu.roll(nb, 1, 1)
    sb = jnp.where(lanes == 0, sa, sb)
    sa = jnp.where(lanes == 0, 0.0, sa)
    here = pl.ds(at, rows)
    co_ref[0, here, :] = east
    co_ref[1, here, :H] = na
    co_ref[1, here, H:] = jnp.where(lanes == H - 1, 0.0, nb)
    co_ref[2, here, :H] = sa
    co_ref[2, here, H:] = sb
    co_ref[3, here, :] = metric
    west = co_ref[0, pl.ds(at - 1, rows), :]
    faces = east + west + north
    co_ref[4, here, :H] = faces[:, :H] + sa
    co_ref[4, here, H:] = faces[:, H:] + sb


def diagonals(cols_ref, co_ref, k, rows):
    m, f = co_ref[3, pl.ds(k, 1), :], co_ref[4, pl.ds(k, 1), :]
    d, a1, a2 = cols_ref[0, rows, :], cols_ref[1, rows, :], cols_ref[2, rows, :]
    ta, tb = d * m[:, :H] + f[:, :H], d * m[:, H:] + f[:, H:]
    return (ta - a1, tb - a1), (ta - a2, tb - a2)


def groups(levels):
    return [pl.ds(g * G, G) for g in range(levels // G)]


def step1(levels, cols, co, k, r, r_e, r_w, store, d1, d2):
    c = coefficients(co, k)
    for rows in groups(levels):
        first, second = diagonals(cols, co, k, rows)
        put(*d1, rows, first)
        put(*d2, rows, second)
        put(*store, rows, operate(first, halves(*r, rows), halves(*r_e, rows), halves(*r_w, rows), c))


def step_even(levels, cols, which, co, k, y, y_e, y_w, old, diag, store):
    c = coefficients(co, k)
    for rows in groups(levels):
        a, b = operate(halves(*diag, rows), halves(*y, rows), halves(*y_e, rows), halves(*y_w, rows), c)
        beta = cols[which, rows, :]
        oa, ob = halves(*old, rows)
        store(rows, (a + beta * oa, b + beta * ob))


def step3(levels, co, k, y, y_e, y_w, diag, store):
    c = coefficients(co, k)
    for rows in groups(levels):
        put(*store, rows, operate(halves(*diag, rows), halves(*y, rows), halves(*y_e, rows), halves(*y_w, rows), c))


def start(copies):
    for copy in copies:
        copy.start()


def wait(copies):
    for copy in copies:
        copy.wait()


def load_row(flat, block, j, levels):
    at = block * (2 * levels * 8) + j
    return jnp.concatenate([flat[pl.ds(at + h * levels * 8, levels, stride=8), :] for h in range(2)], axis=1)


def store_row(flat, block, j, levels, value):
    at = block * (2 * levels * 8) + j
    for h in range(2):
        flat[pl.ds(at + h * levels * 8, levels, stride=8), :] = value[:, h * H : (h + 1) * H]


def interior(first, last, t0, t1, levels, lon, *refs):
    refs = list(refs)
    take = lambda n: [refs.pop(0) for _ in range(n)]
    x_ref, metric_ref, east_ref, north_ref = take(4)
    if first:
        dep_ref, syn_ref, ana_ref = take(3)
    else:
        cols, ws, wa, r0, u0, y0, w0, e0, g0, _out_in = take(10)
    out_ref, edge_ref, save_ref = take(3)
    if first:
        cols, ws, wa = take(3)
    if not last:
        state = take(6)
    co, cbuf, obuf, zbuf, rr, uu, yy, ww, d1, d2, in_sem, out_sem = take(12)
    assert not refs

    blocks = lon // 8
    b_in0 = 0 if first else t0 // 2
    b_in1 = blocks if last else t1 // 2 + 1
    b_in1 = min(b_in1, blocks)

    def fetch(b):
        return [
            pltpu.make_async_copy(x_ref.at[:, pl.ds(8 * b, 8), pl.ds(h * H, H)], cbuf.at[b - b_in0, h], in_sem.at[h, b - b_in0])
            for h in range(2)
        ]

    b_out0 = 1 if first else (t0 - 1) // 2
    b_out1 = blocks - 1 if last else (t1 - 1) // 2

    def flush(b):
        return [
            pltpu.make_async_copy(
                obuf.at[b - (b_out0 - 1), h], out_ref.at[:, pl.ds(8 * b, 8), pl.ds(h * H, H)], out_sem.at[h, b - b_out0])
            for h in range(2)
        ]

    for b in range(b_in0, b_in1):
        start(fetch(b))

    co[0, pl.ds(0, 8), :] = jnp.zeros((8, 2 * H), jnp.float32)
    fill_coefficients(co, 8, metric_ref[...], east_ref[...], north_ref[...])
    if first:
        prepare(dep_ref, syn_ref, ana_ref, cols, ws, wa)
    else:
        for src, dst in ((r0, rr), (u0, uu), (y0, yy), (w0, ww), (e0, d1), (g0, d2)):
            dst[...] = src[...]

    rows_in = cbuf.reshape(cbuf.shape[0] * 2 * levels * 8, H)
    rows_out = obuf.reshape(obuf.shape[0] * 2 * levels * 8, H)

    wait(fetch(b_in0))
    if first:
        rr[0] = mix(ws[...], load_row(rows_in, 0, 0, levels))
        save_ref[0, 0] = rr[0]

    def finish(row):
        o = jnp.dot(wa[...], zbuf[...], preferred_element_type=jnp.float32)
        b = lax.div(row + 8, 8) - 1 - (b_out0 - 1)
        store_row(rows_out, b, lax.rem(row + 8, 8), levels, o)

    def store_z(rows, pair):
        start = rows.start
        for h in range(2):
            high, low = split(pair[h])
            lanes = slice(h * H, (h + 1) * H)
            zbuf[pl.ds(start, G), lanes] = high
            zbuf[pl.ds(levels + start, G), lanes] = low
            zbuf[pl.ds(2 * levels + start, G), lanes] = high

    def body(t, _):
        b = lax.div(t + 1, 2)

        @pl.when((lax.rem(t, 2) == 1) & (b < b_in1) & (b > b_in0))
        def _():
            wait(fetch(b))

        for s in range(4):
            i = 4 * t + s
            nxt = i + 1
            bb = lax.div(nxt, 8) - b_in0
            finish_row = i - 5
            if first:
                finish_row = jnp.maximum(finish_row, 0)
            finish(finish_row)
            rr[(s + 1) % 4] = mix(ws[...], load_row(rows_in, bb, lax.rem(nxt, 8), levels))
            k = 8 + i
            q = lambda n: (s + n) % 4
            step1(levels, cols, co, k - 1, (rr, q(3)), (rr, q(0)), (rr, q(2)), (uu, q(3)), (d1, q(3)), (d2, q(3)))
            step_even(levels, cols, 3, co, k - 2, (uu, q(2)), (uu, q(3)), (uu, q(1)), (rr, q(2)), (d1, q(2)),
                      lambda rows, pair, at=q(2): put(yy, at, rows, pair))
            step3(levels, co, k - 3, (yy, q(1)), (yy, q(2)), (yy, q(0)), (d2, q(1)), (ww, q(1)))
            step_even(levels, cols, 4, co, k - 4, (ww, q(0)), (ww, q(1)), (ww, q(3)), (yy, q(0)), (d2, q(0)), store_z)

        if first:

            @pl.when(t == 0)
            def _():
                save_ref[0, 1] = rr[1]
                save_ref[1, 0] = uu[1]
                save_ref[1, 1] = uu[2]

            @pl.when(t == 1)
            def _():
                save_ref[2, 0] = yy[2]
                save_ref[2, 1] = yy[3]
                save_ref[3, 0] = ww[3]
                save_ref[3, 1] = ww[0]

        bo = lax.div(t - 3, 2)

        @pl.when((lax.rem(t, 2) == 1) & (t >= 3) & (bo >= b_out0) & (bo < b_out1))
        def _():
            start(flush(bo))

        return 0

    lax.fori_loop(t0, t1, body, 0)
    finish(jnp.int32(4 * t1 - 5))
    if not last:
        start(flush(b_out1 - 1))
        for src, dst in zip((rr, uu, yy, ww, d1, d2), state):
            dst[...] = src[...]
    if first:
        edge_ref[...] = obuf[0]
    else:
        edge_ref[...] = obuf[blocks - 1 - (b_out0 - 1)]
    if last:
        at = 4 * t1
        for f, (ref, row) in enumerate(((rr, at - 2), (uu, at - 3), (yy, at - 4), (ww, at - 5))):
            save_ref[f, 0] = ref[row % 4]
            save_ref[f, 1] = ref[(row + 1) % 4]
    for b in range(b_out0, b_out1):
        wait(flush(b))


def edges(levels, lon, *refs):
    (hl, hr, metric_ref, east_ref, north_ref, cols, ws, wa, save_l, save_r, edge_l, edge_r, _out_in,
     out_ref, co, rr, uu, yy, ww, d1, d2, zbuf, obuf, sems) = refs
    copies = []
    for side in range(2):
        halo = hr if side else hl
        c = co.at[side]
        c[0, pl.ds(0, 8), :] = jnp.zeros((8, 2 * H), jnp.float32)
        own = pl.ds(lon - 8, 8) if side else pl.ds(0, 8)
        mine = (metric_ref[own, :], east_ref[own, :], north_ref[own, :])
        theirs = [halo[:, levels + f, :] for f in range(3)]
        if side:
            window = [jnp.concatenate([a, b], axis=0) for a, b in zip(mine, theirs)]
            base = 8 + 4
        else:
            window = [jnp.concatenate([b, a], axis=0) for a, b in zip(mine, theirs)]
            base = 8
        fill_coefficients(c, 8, *window)
        r, u, y, w = rr.at[side], uu.at[side], yy.at[side], ww.at[side]
        e, g = d1.at[side], d2.at[side]
        save = save_r if side else save_l
        edge = edge_r if side else edge_l
        new_r = 4 if side else 0
        for j in range(4):
            r[new_r + j] = mix(ws[...], halo[j, :levels, :])
        u0, y0, w0, z0 = (3, 2, 1, 0) if side else (1, 2, 3, 4)
        old_r, old_u, old_y, old_w = (2, 1, 0, -1) if side else (4, 5, 6, 7)
        for f, (ref, row) in enumerate(((r, old_r), (u, old_u), (y, old_y), (w, old_w + 1))):
            ref[row] = save[f, 0]
            ref[row + 1] = save[f, 1]
        for n in range(0, 4) if side else range(4, 8):
            if not (u0 <= n < u0 + 4):
                for rows in groups(levels):
                    first, second = diagonals(cols, c, base + n, rows)
                    put(e, n, rows, first)
                    put(g, n, rows, second)
        for j in range(4):
            n = u0 + j
            step1(levels, cols, c, base + n, (r, n), (r, n + 1), (r, n - 1), (u, n), (e, n), (g, n))
        for j in range(4):
            n = y0 + j
            step_even(levels, cols, 3, c, base + n, (u, n), (u, n + 1), (u, n - 1), (r, n), (e, n),
                      lambda rows, pair, n=n: put(y, n, rows, pair))
        for j in range(4):
            n = w0 + j
            step3(levels, c, base + n, (y, n), (y, n + 1), (y, n - 1), (g, n), (w, n + 1))
        ob = obuf.at[side]
        ob[...] = edge[...]
        flat = ob.reshape(2 * levels * 8, H)
        for j in range(4):
            n = z0 + j
            z = zbuf.at[side, j]

            def store_z(rows, pair, z=z):
                start = rows.start
                for h in range(2):
                    high, low = split(pair[h])
                    lanes = slice(h * H, (h + 1) * H)
                    z[pl.ds(start, G), lanes] = high
                    z[pl.ds(levels + start, G), lanes] = low
                    z[pl.ds(2 * levels + start, G), lanes] = high

            step_even(levels, cols, 4, c, base + n, (w, n + 1), (w, n + 2), (w, n), (y, n), (g, n), store_z)
            o = jnp.dot(wa[...], z[...], preferred_element_type=jnp.float32)
            store_row(flat, 0, (4 + j) if side else j, levels, o)
        at = lon - 8 if side else 0
        for h in range(2):
            copies.append(pltpu.make_async_copy(ob.at[h], out_ref.at[:, pl.ds(at, 8), pl.ds(h * H, H)], sems.at[side, h]))
        start(copies[-2:])
    wait(copies)


F32, BF16 = jnp.float32, jnp.bfloat16
ANY = pl.BlockSpec(memory_space=pl.ANY)
VM = pl.BlockSpec(memory_space=pltpu.VMEM)


def shape(*dims, dtype=F32):
    return jax.ShapeDtypeStruct(dims, dtype)


def run_interior(first, last, t0, t1, levels, lon, lat, args, state, out_prev):
    ring = lambda: pltpu.VMEM((4, levels, lat), F32)
    outs = [(shape(levels, lon, lat), ANY), (shape(2, levels, 8, H), VM), (shape(4, 2, levels, lat), VM)]
    if first:
        outs += [(shape(5, levels, H), VM), (shape(levels, 3 * levels, dtype=BF16), VM), (shape(levels, 3 * levels, dtype=BF16), VM)]
    if not last:
        outs += [(shape(4, levels, lat), VM)] * 6
    blocks = lon // 8
    operands = list(args) + list(state)
    specs = [ANY] + [VM] * (len(operands) - 1)
    aliases = {}
    if out_prev is not None:
        aliases[len(operands)] = 0
        operands.append(out_prev)
        specs.append(ANY)
    return pl.pallas_call(
        functools.partial(interior, first, last, t0, t1, levels, lon),
        out_shape=[o for o, _ in outs],
        in_specs=specs,
        out_specs=[s for _, s in outs],
        input_output_aliases=aliases,
        scratch_shapes=[
            pltpu.VMEM((5, lon + 8, lat), F32),
            pltpu.VMEM((blocks + 1, 2, levels, 8, H), F32),
            pltpu.VMEM((blocks + 1, 2, levels, 8, H), F32),
            pltpu.VMEM((3 * levels, lat), BF16),
            ring(), ring(), ring(), ring(), ring(), ring(),
            pltpu.SemaphoreType.DMA((2, blocks + 1)),
            pltpu.SemaphoreType.DMA((2, blocks + 1)),
        ],
        compiler_params=pltpu.CompilerParams(vmem_limit_bytes=VMEM_LIMIT),
        name="interior",
    )(*operands)


def run_edges(levels, lon, lat, operands):
    return pl.pallas_call(
        functools.partial(edges, levels, lon),
        out_shape=shape(levels, lon, lat),
        in_specs=[VM] * 12 + [ANY],
        out_specs=ANY,
        input_output_aliases={12: 0},
        scratch_shapes=[
            pltpu.VMEM((2, 5, 24, lat), F32),
            pltpu.VMEM((2, 8, levels, lat), F32),
            pltpu.VMEM((2, 8, levels, lat), F32),
            pltpu.VMEM((2, 8, levels, lat), F32),
            pltpu.VMEM((2, 10, levels, lat), F32),
            pltpu.VMEM((2, 8, levels, lat), F32),
            pltpu.VMEM((2, 8, levels, lat), F32),
            pltpu.VMEM((2, 4, 3 * levels, lat), BF16),
            pltpu.VMEM((2, 2, levels, 8, H), F32),
            pltpu.SemaphoreType.DMA((2, 2)),
        ],
        compiler_params=pltpu.CompilerParams(vmem_limit_bytes=VMEM_LIMIT),
        name="edges",
    )(*operands)


def message(x, coeffs, lo, hi):
    return jnp.concatenate([x[:, lo:hi, :].transpose(1, 0, 2), jnp.stack([c[lo:hi] for c in coeffs], axis=1)], axis=1)


def shards(cotangent, synthesis, analysis, depths, metric, east_face, north_face):
    levels, lon, lat = cotangent.shape
    coeffs = (metric, east_face, north_face)
    count = lax.axis_size("lon")
    from_west = lax.ppermute(message(cotangent, coeffs, lon - 4, lon), "lon", [(i, (i + 1) % count) for i in range(count)])
    from_east = lax.ppermute(message(cotangent, coeffs, 0, 4), "lon", [((i + 1) % count, i) for i in range(count)])
    args = (cotangent,) + coeffs
    out, edge_l, save_l, cols, ws, wa, *state = run_interior(
        True, False, 0, 7, levels, lon, lat, args + (depths.reshape(1, -1), synthesis, analysis), (), None)
    out, edge_r, save_r = run_interior(False, True, 7, lon // 4, levels, lon, lat, args, (cols, ws, wa, *state), out)
    return run_edges(levels, lon, lat, (from_west, from_east) + coeffs + (cols, ws, wa, save_l, save_r, edge_l, edge_r, out))


def solution(mesh):
    placed = (P(None, ("parts", "lon"), None), P(), P(), P(), P("lon", None), P("lon", None), P("lon", None))
    return jax.shard_map(
        shards, mesh=mesh, in_specs=placed, out_specs=P(None, ("parts", "lon"), None), check_vma=False)
```

```python
import functools
import math

import jax
import jax.numpy as jnp
from jax import lax
from jax.experimental import pallas as pl
from jax.experimental.pallas import tpu as pltpu
from jax.sharding import PartitionSpec as P

G = 16
H = 128
LIM_A, LIM_B = 28, 24
EARLY, LATE = 4, 6
COS1, COS2 = math.cos(2 * math.pi / 5), math.cos(4 * math.pi / 5)
SIN1, SIN2 = math.sin(2 * math.pi / 5) ** 2, math.sin(4 * math.pi / 5) ** 2


def column(row):
    n = row.shape[1]
    eye = lax.broadcasted_iota(jnp.int32, (n, n), 0) == lax.broadcasted_iota(jnp.int32, (n, n), 1)
    picked = jnp.sum(jnp.where(eye, jnp.broadcast_to(row, (n, n)), 0.0), axis=1, keepdims=True)
    return jnp.broadcast_to(picked, (n, H))


def split(x):
    high = x.astype(jnp.bfloat16)
    low = (x - high.astype(jnp.float32)).astype(jnp.bfloat16)
    return high, low


def prepare(small, at, cols_ref, ws_ref, wa_ref):
    n = ws_ref.shape[0]
    row = small[pl.ds(at + 2 * n, 1), :n]
    centre = 1.25 * row + 4.0
    half = 0.75 * row + 4.0
    product = row * (row + 4.0)
    c2, h2 = centre * centre, half * half
    gain = 16.0 / (centre * (16.0 * c2 * c2 - 20.0 * c2 * h2 + 5.0 * h2 * h2))
    d = column(row)
    cols_ref[0] = d
    cols_ref[1] = (1.0 - COS1) * (1.25 * d + 4.0)
    cols_ref[2] = (1.0 - COS2) * (1.25 * d + 4.0)
    cols_ref[3] = SIN1 * (d * (d + 4.0))
    cols_ref[4] = SIN2 * (d * (d + 4.0))
    for src, dst, scale in ((small[at : at + n, :n].T, ws_ref, None), (small[at + n : at + 2 * n, :n].T, wa_ref, gain)):
        if scale is not None:
            src = src * scale
        high, low = split(src)
        dst[:, :n] = high
        dst[:, n : 2 * n] = high
        dst[:, 2 * n :] = low


def mix(weights, field):
    high, low = split(field)
    stacked = jnp.concatenate([high, low, high], axis=0)
    return jnp.dot(weights, stacked, preferred_element_type=jnp.float32)


def halves(ref, slot, rows):
    return ref[slot, rows, :H], ref[slot, rows, H:]


def put(ref, slot, rows, pair):
    ref[slot, rows, :H] = pair[0]
    ref[slot, rows, H:] = pair[1]


def coefficients(co_ref, k):
    e = co_ref[0, pl.ds(k, 1), :]
    w = co_ref[0, pl.ds(k - 1, 1), :]
    n = co_ref[1, pl.ds(k, 1), :]
    s = co_ref[2, pl.ds(k, 1), :]
    return tuple((c[:, :H], c[:, H:]) for c in (e, w, n, s))


def operate(diag, y, east, west, co):
    lanes = lax.broadcasted_iota(jnp.int32, (G, H), 1)
    (ea, eb), (wa, wb), (na, nb), (sa, sb) = co
    ya, yb = y
    na_r, nb_r = pltpu.roll(ya, H - 1, 1), pltpu.roll(yb, H - 1, 1)
    sa_r, sb_r = pltpu.roll(ya, 1, 1), pltpu.roll(yb, 1, 1)
    na_r = jnp.where(lanes == H - 1, nb_r, na_r)
    sb_r = jnp.where(lanes == 0, sa_r, sb_r)
    a = (diag[0] * ya - ea * east[0]) - (wa * west[0] + na * na_r + sa * sa_r)
    b = (diag[1] * yb - eb * east[1]) - (wb * west[1] + nb * nb_r + sb * sb_r)
    return a, b


def fill_coefficients(co_ref, at, metric, east, north):
    rows = metric.shape[0]
    lanes = lax.broadcasted_iota(jnp.int32, (rows, H), 1)
    na, nb = north[:, :H], north[:, H:]
    sa, sb = pltpu.roll(na, 1, 1), pltpu.roll(nb, 1, 1)
    sb = jnp.where(lanes == 0, sa, sb)
    sa = jnp.where(lanes == 0, 0.0, sa)
    here = pl.ds(at, rows)
    co_ref[0, here, :] = east
    co_ref[1, here, :H] = na
    co_ref[1, here, H:] = jnp.where(lanes == H - 1, 0.0, nb)
    co_ref[2, here, :H] = sa
    co_ref[2, here, H:] = sb
    co_ref[3, here, :] = metric
    west = co_ref[0, pl.ds(at - 1, rows), :]
    faces = east + west + north
    co_ref[4, here, :H] = faces[:, :H] + sa
    co_ref[4, here, H:] = faces[:, H:] + sb


def diagonals(cols_ref, co_ref, k, rows):
    m, f = co_ref[3, pl.ds(k, 1), :], co_ref[4, pl.ds(k, 1), :]
    d, a1, a2 = cols_ref[0, rows, :], cols_ref[1, rows, :], cols_ref[2, rows, :]
    ta, tb = d * m[:, :H] + f[:, :H], d * m[:, H:] + f[:, H:]
    return (ta - a1, tb - a1), (ta - a2, tb - a2)


def groups(levels):
    return [pl.ds(g * G, G) for g in range(levels // G)]


def step1(levels, cols, co, k, r, r_e, r_w, store, d1, d2):
    c = coefficients(co, k)
    for rows in groups(levels):
        first, second = diagonals(cols, co, k, rows)
        put(*d1, rows, first)
        put(*d2, rows, second)
        put(*store, rows, operate(first, halves(*r, rows), halves(*r_e, rows), halves(*r_w, rows), c))


def step_even(levels, cols, which, co, k, y, y_e, y_w, old, diag, store):
    c = coefficients(co, k)
    for rows in groups(levels):
        a, b = operate(halves(*diag, rows), halves(*y, rows), halves(*y_e, rows), halves(*y_w, rows), c)
        beta = cols[which, rows, :]
        oa, ob = halves(*old, rows)
        store(rows, (a + beta * oa, b + beta * ob))


def step3(levels, co, k, y, y_e, y_w, diag, store):
    c = coefficients(co, k)
    for rows in groups(levels):
        put(*store, rows, operate(halves(*diag, rows), halves(*y, rows), halves(*y_e, rows), halves(*y_w, rows), c))


def start(copies):
    for copy in copies:
        copy.start()


def wait(copies):
    for copy in copies:
        copy.wait()


def load_row(flat, block, j, levels):
    at = block * (2 * levels * 8) + j
    return jnp.concatenate([flat[pl.ds(at + h * levels * 8, levels, stride=8), :] for h in range(2)], axis=1)


def store_row(flat, block, j, levels, value):
    at = block * (2 * levels * 8) + j
    for h in range(2):
        flat[pl.ds(at + h * levels * 8, levels, stride=8), :] = value[:, h * H : (h + 1) * H]


RESUME = (("r", (2, 3, 0)), ("u", (1, 2)), ("y", (0, 1)), ("w", (3, 0)), ("d1", (2,)), ("d2", (0, 1, 2)))
CARRIED = sum(len(slots) for _, slots in RESUME)


def interior(first, early, late, levels, lon, *refs):
    refs = list(refs)
    take = lambda n: [refs.pop(0) for _ in range(n)]
    blocks = lon // 8
    stop = jnp.where(lax.axis_index("lon") == 0, late, early)
    half = lax.div(stop, 2)
    if first:
        x_ref, small = take(2)
        save_ref, cols, ws, wa, co, to_west, to_east, carried, cbuf, obuf, zbuf = take(11)
        (in_sem,) = take(1)
    else:
        cols, ws, wa, co, carried, cbuf, done, z_in = take(8)
        out_ref, edge_ref, save_ref = take(3)
        obuf, zbuf, out_sem = take(3)
    rr, uu, yy, ww, d1, d2 = take(6)
    assert not refs
    rings = {"r": rr, "u": uu, "y": yy, "w": ww, "d1": d1, "d2": d2}

    def fetch(b):
        return [
            pltpu.make_async_copy(x_ref.at[:, pl.ds(8 * b, 8), pl.ds(h * H, H)], cbuf.at[b, h], in_sem.at[h, b])
            for h in range(2)
        ]

    def flush(src, b):
        return [
            pltpu.make_async_copy(src.at[b, h], out_ref.at[:, pl.ds(8 * b, 8), pl.ds(h * H, H)], out_sem.at[h, b])
            for h in range(2)
        ]

    if first:
        for b in range(blocks):
            start(fetch(b))

    rows_in = cbuf.reshape(cbuf.shape[0] * 2 * levels * 8, H)
    rows_out = obuf.reshape(obuf.shape[0] * 2 * levels * 8, H)
    if first:
        prepare(small, 3 * lon, cols, ws, wa)
        co[0, pl.ds(0, 8), :] = jnp.zeros((8, 2 * H), jnp.float32)
        fill_coefficients(co, 8, *(small[f * lon : (f + 1) * lon, :] for f in range(3)))
        wait(fetch(0))
        rr[0] = mix(ws[...], load_row(rows_in, 0, 0, levels))
        save_ref[0, 0] = rr[0]
    else:
        lax.fori_loop(1, half - 1, lambda b, _: (start(flush(done, b)), 0)[1], 0)
        n = 0
        for name, slots in RESUME:
            for slot in slots:
                rings[name][slot] = carried[n]
                n += 1
        zbuf[...] = z_in[...]
        obuf[half - 1] = done[half - 1]

    def finish(row):
        o = jnp.dot(wa[...], zbuf[...], preferred_element_type=jnp.float32)
        store_row(rows_out, lax.div(row, 8), lax.rem(row, 8), levels, o)

    def store_z(rows, pair):
        start = rows.start
        for h in range(2):
            high, low = split(pair[h])
            lanes = slice(h * H, (h + 1) * H)
            zbuf[pl.ds(start, G), lanes] = high
            zbuf[pl.ds(levels + start, G), lanes] = low
            zbuf[pl.ds(2 * levels + start, G), lanes] = high

    def body(t, _):
        if first:
            b = lax.div(t + 1, 2)

            @pl.when((lax.rem(t, 2) == 1) & (b < blocks))
            def _():
                wait(fetch(b))

        for s in range(4):
            i = 4 * t + s
            nxt = i + 1
            finish(jnp.maximum(i - 5, 0) if first else i - 5)
            rr[(s + 1) % 4] = mix(ws[...], load_row(rows_in, lax.div(nxt, 8), lax.rem(nxt, 8), levels))
            k = 8 + i
            q = lambda n: (s + n) % 4
            step1(levels, cols, co, k - 1, (rr, q(3)), (rr, q(0)), (rr, q(2)), (uu, q(3)), (d1, q(3)), (d2, q(3)))
            step_even(levels, cols, 3, co, k - 2, (uu, q(2)), (uu, q(3)), (uu, q(1)), (rr, q(2)), (d1, q(2)),
                      lambda rows, pair, at=q(2): put(yy, at, rows, pair))
            step3(levels, co, k - 3, (yy, q(1)), (yy, q(2)), (yy, q(0)), (d2, q(1)), (ww, q(1)))
            step_even(levels, cols, 4, co, k - 4, (ww, q(0)), (ww, q(1)), (ww, q(3)), (yy, q(0)), (d2, q(0)), store_z)

        if first:

            @pl.when(t == 0)
            def _():
                save_ref[0, 1] = rr[1]
                save_ref[1, 0] = uu[1]
                save_ref[1, 1] = uu[2]

            @pl.when(t == 1)
            def _():
                save_ref[2, 0] = yy[2]
                save_ref[2, 1] = yy[3]
                save_ref[3, 0] = ww[3]
                save_ref[3, 1] = ww[0]

        if not first:
            bo = lax.div(t - 3, 2)

            @pl.when((lax.rem(t, 2) == 1) & (bo >= 1) & (bo < blocks - 2))
            def _():
                start(flush(obuf, bo))

        return 0

    if first:
        lax.fori_loop(0, stop, body, 0)
        n = 0
        for name, slots in RESUME:
            for slot in slots:
                carried[n] = rings[name][slot]
                n += 1
        lax.fori_loop(half + 1, blocks, lambda b, _: (wait(fetch(b)), 0)[1], 0)
        for j in range(8):
            msg_ref = (to_west, to_east)[j // 4]
            block, row = ((0, j), (blocks - 1, j))[j // 4]
            at = j if j < 4 else lon - 8 + j
            msg_ref[j % 4, :levels, :] = load_row(rows_in, block, row, levels)
            for f in range(3):
                msg_ref[j % 4, pl.ds(levels + f, 1), :] = small[pl.ds(f * lon + at, 1), :]
    else:
        lax.fori_loop(stop, lon // 4, body, 0)
        finish(lon - 5)
        edge_ref[0] = obuf[blocks - 2]
        edge_ref[1] = obuf[blocks - 1]
        for f, (ref, row) in enumerate(((rr, lon - 2), (uu, lon - 3), (yy, lon - 4), (ww, lon - 5))):
            save_ref[f, 0] = ref[row % 4]
            save_ref[f, 1] = ref[(row + 1) % 4]
        lax.fori_loop(1, blocks - 2, lambda b, _: (wait(flush(obuf, b)), 0)[1], 0)


def edges(levels, lon, *refs):
    (hl, hr, small, cols, ws, wa, save_l, save_r, edge_l, edge_r, _out_in,
     out_ref, co, rr, uu, yy, ww, d1, d2, zbuf, obuf, sems) = refs
    copies = [
        pltpu.make_async_copy(edge_r.at[0, h], out_ref.at[:, pl.ds(lon - 16, 8), pl.ds(h * H, H)], sems.at[2, h])
        for h in range(2)
    ]
    start(copies)
    for side in range(2):
        halo = hr if side else hl
        c = co.at[side]
        c[0, pl.ds(0, 8), :] = jnp.zeros((8, 2 * H), jnp.float32)
        own = lon - 8 if side else 0
        mine = tuple(small[pl.ds(f * lon + own, 8), :] for f in range(3))
        theirs = [halo[:, levels + f, :] for f in range(3)]
        if side:
            window = [jnp.concatenate([a, b], axis=0) for a, b in zip(mine, theirs)]
            base = 8 + 4
        else:
            window = [jnp.concatenate([b, a], axis=0) for a, b in zip(mine, theirs)]
            base = 8
        fill_coefficients(c, 8, *window)
        r, u, y, w = rr.at[side], uu.at[side], yy.at[side], ww.at[side]
        e, g = d1.at[side], d2.at[side]
        save = save_r if side else save_l
        edge = edge_r.at[1] if side else edge_l.at[0]
        new_r = 4 if side else 0
        for j in range(4):
            r[new_r + j] = mix(ws[...], halo[j, :levels, :])
        u0, y0, w0, z0 = (3, 2, 1, 0) if side else (1, 2, 3, 4)
        old_r, old_u, old_y, old_w = (2, 1, 0, -1) if side else (4, 5, 6, 7)
        for f, (ref, row) in enumerate(((r, old_r), (u, old_u), (y, old_y), (w, old_w + 1))):
            ref[row] = save[f, 0]
            ref[row + 1] = save[f, 1]
        for n in range(0, 4) if side else range(4, 8):
            if not (u0 <= n < u0 + 4):
                for rows in groups(levels):
                    first, second = diagonals(cols, c, base + n, rows)
                    put(e, n, rows, first)
                    put(g, n, rows, second)
        for j in range(4):
            n = u0 + j
            step1(levels, cols, c, base + n, (r, n), (r, n + 1), (r, n - 1), (u, n), (e, n), (g, n))
        for j in range(4):
            n = y0 + j
            step_even(levels, cols, 3, c, base + n, (u, n), (u, n + 1), (u, n - 1), (r, n), (e, n),
                      lambda rows, pair, n=n: put(y, n, rows, pair))
        for j in range(4):
            n = w0 + j
            step3(levels, c, base + n, (y, n), (y, n + 1), (y, n - 1), (g, n), (w, n + 1))
        ob = obuf.at[side]
        ob[...] = edge[...]
        flat = ob.reshape(2 * levels * 8, H)
        for j in range(4):
            n = z0 + j
            z = zbuf.at[side, j]

            def store_z(rows, pair, z=z):
                start = rows.start
                for h in range(2):
                    high, low = split(pair[h])
                    lanes = slice(h * H, (h + 1) * H)
                    z[pl.ds(start, G), lanes] = high
                    z[pl.ds(levels + start, G), lanes] = low
                    z[pl.ds(2 * levels + start, G), lanes] = high

            step_even(levels, cols, 4, c, base + n, (w, n + 1), (w, n + 2), (w, n), (y, n), (g, n), store_z)
            o = jnp.dot(wa[...], z[...], preferred_element_type=jnp.float32)
            store_row(flat, 0, (4 + j) if side else j, levels, o)
        at = lon - 8 if side else 0
        for h in range(2):
            copies.append(pltpu.make_async_copy(ob.at[h], out_ref.at[:, pl.ds(at, 8), pl.ds(h * H, H)], sems.at[side, h]))
        start(copies[-2:])
    wait(copies)


F32, BF16 = jnp.float32, jnp.bfloat16
HBM = pl.BlockSpec(memory_space=pltpu.HBM)
ANY = pl.BlockSpec(memory_space=pl.ANY)
VM = pl.BlockSpec(memory_space=pltpu.VMEM)


def shape(*dims, dtype=F32):
    return jax.ShapeDtypeStruct(dims, dtype)


def params(mib):
    return pltpu.CompilerParams(vmem_limit_bytes=mib * 1024 * 1024)


def run_interior(first, levels, lon, lat, operands):
    ring = pltpu.VMEM((4, levels, lat), F32)
    blocks = lon // 8
    mixer = shape(levels, 3 * levels, dtype=BF16)
    saved = shape(4, 2, levels, lat)
    if first:
        outs = [saved, shape(5, levels, H), mixer, mixer, shape(5, lon + 8, lat), shape(4, levels + 8, lat), shape(4, levels + 8, lat),
                shape(CARRIED, levels, lat), shape(blocks + 1, 2, levels, 8, H), shape(LATE // 2, 2, levels, 8, H),
                shape(3 * levels, lat, dtype=BF16)]
        in_specs = [HBM, VM]
        out_specs = [VM] * len(outs)
        scratch = [pltpu.SemaphoreType.DMA((2, blocks))]
    else:
        outs = [shape(levels, lon, lat), shape(2, 2, levels, 8, H), saved]
        in_specs = [VM] * 8
        out_specs = [HBM, VM, VM]
        scratch = [pltpu.VMEM((blocks, 2, levels, 8, H), F32), pltpu.VMEM((3 * levels, lat), BF16),
                   pltpu.SemaphoreType.DMA((2, blocks))]
    return pl.pallas_call(
        functools.partial(interior, first, EARLY, LATE, levels, lon),
        out_shape=outs,
        in_specs=in_specs,
        out_specs=out_specs,
        scratch_shapes=scratch + [ring, ring, ring, ring, ring, ring],
        compiler_params=params(LIM_A if first else LIM_B),
        name="interior",
    )(*operands)


def run_edges(levels, lon, lat, operands):
    window = lambda n: pltpu.VMEM((2, n, levels, lat), F32)
    return pl.pallas_call(
        functools.partial(edges, levels, lon),
        out_shape=shape(levels, lon, lat),
        in_specs=[VM] * 10 + [HBM],
        out_specs=HBM,
        input_output_aliases={10: 0},
        scratch_shapes=[
            pltpu.VMEM((2, 5, 24, lat), F32),
            window(8), window(8), window(8), window(10), window(8), window(8),
            pltpu.VMEM((2, 4, 3 * levels, lat), BF16),
            pltpu.VMEM((2, 2, levels, 8, H), F32),
            pltpu.SemaphoreType.DMA((3, 2)),
        ],
        compiler_params=params(LIM_B),
        name="edges",
    )(*operands)


def shards(cotangent, synthesis, analysis, depths, metric, east_face, north_face):
    levels, lon, lat = cotangent.shape
    count = lax.axis_size("lon")
    parts = [metric, east_face, north_face, synthesis, analysis, depths[None]]
    total = 3 * lon + 2 * levels + 8
    small, at = 0.0, 0
    for part in parts:
        rows, width = part.shape
        small = small + jnp.pad(part, ((at, total - at - rows), (0, lat - width)))
        at += rows
    save_l, cols, ws, wa, co, to_west, to_east, carried, blocks_in, blocks_out, z = run_interior(
        True, levels, lon, lat, (cotangent, small))
    from_west = lax.ppermute(to_east, "lon", [(i, (i + 1) % count) for i in range(count)])
    from_east = lax.ppermute(to_west, "lon", [((i + 1) % count, i) for i in range(count)])
    out, edge_r, save_r = run_interior(
        False, levels, lon, lat, (cols, ws, wa, co, carried, blocks_in, blocks_out, z))
    return run_edges(levels, lon, lat, (from_west, from_east, small, cols, ws, wa, save_l, save_r, blocks_out, edge_r, out))


def solution(mesh):
    placed = (P(None, ("parts", "lon"), None), P(), P(), P(), P("lon", None), P("lon", None), P("lon", None))
    return jax.shard_map(
        shards, mesh=mesh, in_specs=placed, out_specs=P(None, ("parts", "lon"), None), check_vma=False)
```

```python
import functools
import math

import jax
import jax.numpy as jnp
from jax import lax
from jax.experimental import pallas as pl
from jax.experimental.pallas import tpu as pltpu
from jax.sharding import PartitionSpec as P

G = 16
H = 128
LIM_A, LIM_B = 28, 24
EARLY, LATE = 2, 3
COS1, COS2 = math.cos(2 * math.pi / 5), math.cos(4 * math.pi / 5)
SIN1, SIN2 = math.sin(2 * math.pi / 5) ** 2, math.sin(4 * math.pi / 5) ** 2


def column(row):
    n = row.shape[1]
    eye = lax.broadcasted_iota(jnp.int32, (n, n), 0) == lax.broadcasted_iota(jnp.int32, (n, n), 1)
    picked = jnp.sum(jnp.where(eye, jnp.broadcast_to(row, (n, n)), 0.0), axis=1, keepdims=True)
    return jnp.broadcast_to(picked, (n, H))


def split(x):
    high = x.astype(jnp.bfloat16)
    low = (x - high.astype(jnp.float32)).astype(jnp.bfloat16)
    return high, low


def prepare(lon, small, cols_ref, ws_ref, wa_ref, co):
    at = 3 * lon
    co[0, pl.ds(0, 8), :] = jnp.zeros((8, 2 * H), jnp.float32)
    fill_coefficients(co, 8, *(small[f * lon : (f + 1) * lon, :] for f in range(3)))
    n = ws_ref.shape[0]
    row = small[pl.ds(at + 2 * n, 1), :n]
    centre = 1.25 * row + 4.0
    half = 0.75 * row + 4.0
    product = row * (row + 4.0)
    c2, h2 = centre * centre, half * half
    gain = 16.0 / (centre * (16.0 * c2 * c2 - 20.0 * c2 * h2 + 5.0 * h2 * h2))
    d = column(row)
    cols_ref[0] = d
    cols_ref[1] = (1.0 - COS1) * (1.25 * d + 4.0)
    cols_ref[2] = (1.0 - COS2) * (1.25 * d + 4.0)
    cols_ref[3] = SIN1 * (d * (d + 4.0))
    cols_ref[4] = SIN2 * (d * (d + 4.0))
    for src, dst, scale in ((small[at : at + n, :n].T, ws_ref, None), (small[at + n : at + 2 * n, :n].T, wa_ref, gain)):
        if scale is not None:
            src = src * scale
        high, low = split(src)
        dst[:, :n] = high
        dst[:, n : 2 * n] = high
        dst[:, 2 * n :] = low


def mix(weights, field):
    high, low = split(field)
    stacked = jnp.concatenate([high, low, high], axis=0)
    return jnp.dot(weights, stacked, preferred_element_type=jnp.float32)


def halves(ref, slot, rows):
    return ref[slot, rows, :H], ref[slot, rows, H:]


def put(ref, slot, rows, pair):
    ref[slot, rows, :H] = pair[0]
    ref[slot, rows, H:] = pair[1]


def coefficients(co_ref, k):
    e = co_ref[0, pl.ds(k, 1), :]
    w = co_ref[0, pl.ds(k - 1, 1), :]
    n = co_ref[1, pl.ds(k, 1), :]
    s = co_ref[2, pl.ds(k, 1), :]
    return tuple((c[:, :H], c[:, H:]) for c in (e, w, n, s))


def operate(diag, y, east, west, co):
    lanes = lax.broadcasted_iota(jnp.int32, (G, H), 1)
    (ea, eb), (wa, wb), (na, nb), (sa, sb) = co
    ya, yb = y
    na_r, nb_r = pltpu.roll(ya, H - 1, 1), pltpu.roll(yb, H - 1, 1)
    sa_r, sb_r = pltpu.roll(ya, 1, 1), pltpu.roll(yb, 1, 1)
    na_r = jnp.where(lanes == H - 1, nb_r, na_r)
    sb_r = jnp.where(lanes == 0, sa_r, sb_r)
    a = (diag[0] * ya - ea * east[0]) - (wa * west[0] + na * na_r + sa * sa_r)
    b = (diag[1] * yb - eb * east[1]) - (wb * west[1] + nb * nb_r + sb * sb_r)
    return a, b


def fill_coefficients(co_ref, at, metric, east, north):
    rows = metric.shape[0]
    lanes = lax.broadcasted_iota(jnp.int32, (rows, H), 1)
    na, nb = north[:, :H], north[:, H:]
    sa, sb = pltpu.roll(na, 1, 1), pltpu.roll(nb, 1, 1)
    sb = jnp.where(lanes == 0, sa, sb)
    sa = jnp.where(lanes == 0, 0.0, sa)
    here = pl.ds(at, rows)
    co_ref[0, here, :] = east
    co_ref[1, here, :H] = na
    co_ref[1, here, H:] = jnp.where(lanes == H - 1, 0.0, nb)
    co_ref[2, here, :H] = sa
    co_ref[2, here, H:] = sb
    co_ref[3, here, :] = metric
    west = co_ref[0, pl.ds(at - 1, rows), :]
    faces = east + west + north
    co_ref[4, here, :H] = faces[:, :H] + sa
    co_ref[4, here, H:] = faces[:, H:] + sb


def diagonals(cols_ref, co_ref, k, rows):
    m, f = co_ref[3, pl.ds(k, 1), :], co_ref[4, pl.ds(k, 1), :]
    d, a1, a2 = cols_ref[0, rows, :], cols_ref[1, rows, :], cols_ref[2, rows, :]
    ta, tb = d * m[:, :H] + f[:, :H], d * m[:, H:] + f[:, H:]
    return (ta - a1, tb - a1), (ta - a2, tb - a2)


def add_scaled(pair, scale, old):
    return pair[0] + scale * old[0], pair[1] + scale * old[1]


def groups(levels):
    return [pl.ds(g * G, G) for g in range(levels // G)]


def step1(levels, cols, co, k, r, r_e, r_w, store, d1, d2):
    c = coefficients(co, k)
    for rows in groups(levels):
        first, second = diagonals(cols, co, k, rows)
        put(*d1, rows, first)
        put(*d2, rows, second)
        put(*store, rows, operate(first, halves(*r, rows), halves(*r_e, rows), halves(*r_w, rows), c))


def step_even(levels, cols, which, co, k, y, y_e, y_w, old, diag, store):
    c = coefficients(co, k)
    for rows in groups(levels):
        a, b = operate(halves(*diag, rows), halves(*y, rows), halves(*y_e, rows), halves(*y_w, rows), c)
        beta = cols[which, rows, :]
        oa, ob = halves(*old, rows)
        store(rows, (a + beta * oa, b + beta * ob))


def step3(levels, co, k, y, y_e, y_w, diag, store):
    c = coefficients(co, k)
    for rows in groups(levels):
        put(*store, rows, operate(halves(*diag, rows), halves(*y, rows), halves(*y_e, rows), halves(*y_w, rows), c))


def start(copies):
    for copy in copies:
        copy.start()


def wait(copies):
    for copy in copies:
        copy.wait()


def load_row(flat, block, j, levels):
    at = block * (2 * levels * 8) + j
    return jnp.concatenate([flat[pl.ds(at + h * levels * 8, levels, stride=8), :] for h in range(2)], axis=1)


def store_row(flat, block, j, levels, value):
    at = block * (2 * levels * 8) + j
    for h in range(2):
        flat[pl.ds(at + h * levels * 8, levels, stride=8), :] = value[:, h * H : (h + 1) * H]


RESUME = (("r", (2, 3, 0)), ("u", (1, 2)), ("y", (0, 1)), ("w", (3, 0)), ("d1", (2,)), ("d2", (0, 1, 2)))
CARRIED = sum(len(slots) for _, slots in RESUME)


def interior(first, early, late, levels, lon, *refs):
    refs = list(refs)
    take = lambda n: [refs.pop(0) for _ in range(n)]
    blocks = lon // 8
    stop = jnp.where(lax.axis_index("lon") < 2, late, early)
    if first:
        x_ref, small, cols, ws, wa, co = take(6)
        save_ref, near, far, carried, cbuf, obuf, zbuf = take(7)
        (in_sem,) = take(1)
    else:
        cols, ws, wa, co, carried, cbuf, done, z_in = take(8)
        out_ref, edge_ref, save_ref = take(3)
        obuf, zbuf, out_sem = take(3)
    rr, uu, yy, ww, d1, d2 = take(6)
    assert not refs
    rings = {"r": rr, "u": uu, "y": yy, "w": ww, "d1": d1, "d2": d2}

    def fetch(b):
        return [
            pltpu.make_async_copy(x_ref.at[:, pl.ds(8 * b, 8), pl.ds(h * H, H)], cbuf.at[b, h], in_sem.at[h, b])
            for h in range(2)
        ]

    def flush(src, b):
        return [
            pltpu.make_async_copy(src.at[b, h], out_ref.at[:, pl.ds(8 * b, 8), pl.ds(h * H, H)], out_sem.at[h, b])
            for h in range(2)
        ]

    if first:
        for b in range(blocks):
            start(fetch(b))

    rows_in = cbuf.reshape(cbuf.shape[0] * 2 * levels * 8, H)
    rows_out = obuf.reshape(obuf.shape[0] * 2 * levels * 8, H)
    if first:
        wait(fetch(0))
        rr[0] = mix(ws[...], load_row(rows_in, 0, 0, levels))
        save_ref[0, 0] = rr[0]
    else:
        lax.fori_loop(1, stop - 1, lambda b, _: (start(flush(done, b)), 0)[1], 0)
        n = 0
        for name, slots in RESUME:
            for slot in slots:
                rings[name][slot] = carried[n]
                n += 1
        zbuf[...] = z_in[...]
        obuf[stop - 1] = done[stop - 1]

    def finish(row):
        o = jnp.dot(wa[...], zbuf[...], preferred_element_type=jnp.float32)
        store_row(rows_out, lax.div(row, 8), lax.rem(row, 8), levels, o)

    def store_z(rows, pair):
        start = rows.start
        for h in range(2):
            high, low = split(pair[h])
            lanes = slice(h * H, (h + 1) * H)
            zbuf[pl.ds(start, G), lanes] = high
            zbuf[pl.ds(levels + start, G), lanes] = low
            zbuf[pl.ds(2 * levels + start, G), lanes] = high

    def advance(t, s, stages):
        i = 8 * t + s
        k = 8 + i
        q = lambda n: (s + n) % 4
        if stages == 4:
            finish(i - 5)
        rr[(s + 1) % 4] = mix(ws[...], load_row(rows_in, t + (s + 1) // 8, (s + 1) % 8, levels))
        if not stages:
            return
        for rows in groups(levels):
            c1, c2, c3, c4 = (coefficients(co, k - min(n, stages)) for n in range(1, 5))
            at = lambda ref, n: halves(ref, q(n), rows)
            first_diag, second_diag = diagonals(cols, co, k - 1, rows)
            put(d1, q(3), rows, first_diag)
            put(d2, q(3), rows, second_diag)
            r = at(rr, 2)
            u = operate(first_diag, at(rr, 3), at(rr, 0), r, c1)
            put(uu, q(3), rows, u)
            if stages < 2:
                continue
            y = add_scaled(operate(at(d1, 2), at(uu, 2), u, at(uu, 1), c2), cols[3, rows, :], r)
            put(yy, q(2), rows, y)
            if stages < 3:
                continue
            old = at(yy, 0)
            w = operate(at(d2, 1), at(yy, 1), y, old, c3)
            put(ww, q(1), rows, w)
            if stages < 4:
                continue
            store_z(rows, add_scaled(operate(at(d2, 0), at(ww, 0), w, at(ww, 3), c4), cols[4, rows, :], old))

    def body(t, _):
        if first:

            @pl.when(t + 1 < blocks)
            def _():
                wait(fetch(t + 1))

        for s in range(8):
            advance(t, s, 4)

        if not first:

            @pl.when(t < blocks - 1)
            def _():
                start(flush(obuf, t - 1))

        return 0

    if first:
        wait(fetch(1))
        for s in range(8):
            advance(0, s, s // 2)
            if s == 3:
                save_ref[0, 1] = rr[1]
                save_ref[1, 0] = uu[1]
                save_ref[1, 1] = uu[2]
        save_ref[2, 0] = yy[2]
        save_ref[2, 1] = yy[3]
        save_ref[3, 0] = ww[3]
        save_ref[3, 1] = ww[0]
        lax.fori_loop(1, stop, body, 0)
        n = 0
        for name, slots in RESUME:
            for slot in slots:
                carried[n] = rings[name][slot]
                n += 1
        lax.fori_loop(stop + 1, blocks, lambda b, _: (wait(fetch(b)), 0)[1], 0)
        even = lax.rem(lax.axis_index("lon"), 2) == 0
        for msg_ref, east in ((near, even), (far, jnp.logical_not(even))):
            block, row = jnp.where(east, blocks - 1, 0), jnp.where(east, 4, 0)
            at = jnp.where(east, lon - 4, 0)
            for j in range(4):
                msg_ref[j, :levels, :] = load_row(rows_in, block, row + j, levels)
                for f in range(3):
                    msg_ref[j, pl.ds(levels + f, 1), :] = small[pl.ds(f * lon + at + j, 1), :]
    else:
        lax.fori_loop(stop, blocks, body, 0)
        finish(lon - 5)
        edge_ref[0] = obuf[blocks - 2]
        edge_ref[1] = obuf[blocks - 1]
        for f, (ref, row) in enumerate(((rr, lon - 2), (uu, lon - 3), (yy, lon - 4), (ww, lon - 5))):
            save_ref[f, 0] = ref[row % 4]
            save_ref[f, 1] = ref[(row + 1) % 4]
        lax.fori_loop(1, blocks - 2, lambda b, _: (wait(flush(obuf, b)), 0)[1], 0)


def edges(levels, lon, *refs):
    (near, far, small, cols, ws, wa, save_l, save_r, edge_l, edge_r, _out_in,
     out_ref, co, rr, uu, yy, ww, d1, d2, zbuf, obuf, halos, sems) = refs
    odd = lax.rem(lax.axis_index("lon"), 2)
    halos[1 - odd] = near[...]
    halos[odd] = far[...]
    copies = [
        pltpu.make_async_copy(edge_r.at[0, h], out_ref.at[:, pl.ds(lon - 16, 8), pl.ds(h * H, H)], sems.at[2, h])
        for h in range(2)
    ]
    start(copies)
    for side in range(2):
        halo = halos.at[side]
        c = co.at[side]
        c[0, pl.ds(0, 8), :] = jnp.zeros((8, 2 * H), jnp.float32)
        own = lon - 8 if side else 0
        mine = tuple(small[pl.ds(f * lon + own, 8), :] for f in range(3))
        theirs = [halo[:, levels + f, :] for f in range(3)]
        if side:
            window = [jnp.concatenate([a, b], axis=0) for a, b in zip(mine, theirs)]
            base = 8 + 4
        else:
            window = [jnp.concatenate([b, a], axis=0) for a, b in zip(mine, theirs)]
            base = 8
        fill_coefficients(c, 8, *window)
        r, u, y, w = rr.at[side], uu.at[side], yy.at[side], ww.at[side]
        e, g = d1.at[side], d2.at[side]
        save = save_r if side else save_l
        edge = edge_r.at[1] if side else edge_l.at[0]
        new_r = 4 if side else 0
        for j in range(4):
            r[new_r + j] = mix(ws[...], halo[j, :levels, :])
        u0, y0, w0, z0 = (3, 2, 1, 0) if side else (1, 2, 3, 4)
        old_r, old_u, old_y, old_w = (2, 1, 0, -1) if side else (4, 5, 6, 7)
        for f, (ref, row) in enumerate(((r, old_r), (u, old_u), (y, old_y), (w, old_w + 1))):
            ref[row] = save[f, 0]
            ref[row + 1] = save[f, 1]
        for n in range(0, 4) if side else range(4, 8):
            if not (u0 <= n < u0 + 4):
                for rows in groups(levels):
                    first, second = diagonals(cols, c, base + n, rows)
                    put(e, n, rows, first)
                    put(g, n, rows, second)
        for j in range(4):
            n = u0 + j
            step1(levels, cols, c, base + n, (r, n), (r, n + 1), (r, n - 1), (u, n), (e, n), (g, n))
        for j in range(4):
            n = y0 + j
            step_even(levels, cols, 3, c, base + n, (u, n), (u, n + 1), (u, n - 1), (r, n), (e, n),
                      lambda rows, pair, n=n: put(y, n, rows, pair))
        for j in range(4):
            n = w0 + j
            step3(levels, c, base + n, (y, n), (y, n + 1), (y, n - 1), (g, n), (w, n + 1))
        ob = obuf.at[side]
        ob[...] = edge[...]
        flat = ob.reshape(2 * levels * 8, H)
        for j in range(4):
            n = z0 + j
            z = zbuf.at[side, j]

            def store_z(rows, pair, z=z):
                start = rows.start
                for h in range(2):
                    high, low = split(pair[h])
                    lanes = slice(h * H, (h + 1) * H)
                    z[pl.ds(start, G), lanes] = high
                    z[pl.ds(levels + start, G), lanes] = low
                    z[pl.ds(2 * levels + start, G), lanes] = high

            step_even(levels, cols, 4, c, base + n, (w, n + 1), (w, n + 2), (w, n), (y, n), (g, n), store_z)
            o = jnp.dot(wa[...], z[...], preferred_element_type=jnp.float32)
            store_row(flat, 0, (4 + j) if side else j, levels, o)
        at = lon - 8 if side else 0
        for h in range(2):
            copies.append(pltpu.make_async_copy(ob.at[h], out_ref.at[:, pl.ds(at, 8), pl.ds(h * H, H)], sems.at[side, h]))
        start(copies[-2:])
    wait(copies)


F32, BF16 = jnp.float32, jnp.bfloat16
HBM = pl.BlockSpec(memory_space=pltpu.HBM)
ANY = pl.BlockSpec(memory_space=pl.ANY)
VM = pl.BlockSpec(memory_space=pltpu.VMEM)


def shape(*dims, dtype=F32):
    return jax.ShapeDtypeStruct(dims, dtype)


def params(mib):
    return pltpu.CompilerParams(vmem_limit_bytes=mib * 1024 * 1024)


def run_prepare(levels, lon, lat, small):
    mixer = shape(levels, 3 * levels, dtype=BF16)
    return pl.pallas_call(
        functools.partial(prepare, lon),
        out_shape=[shape(5, levels, H), mixer, mixer, shape(5, lon + 8, lat)],
        in_specs=[VM],
        out_specs=[VM] * 4,
        compiler_params=params(16),
        cost_estimate=pl.CostEstimate(flops=2 * 10**9, bytes_accessed=2**20, transcendentals=0),
        name="prepare",
    )(small)


def run_interior(first, levels, lon, lat, operands):
    ring = pltpu.VMEM((4, levels, lat), F32)
    blocks = lon // 8
    saved = shape(4, 2, levels, lat)
    if first:
        outs = [saved, shape(4, levels + 8, lat), shape(4, levels + 8, lat),
                shape(CARRIED, levels, lat), shape(blocks + 1, 2, levels, 8, H), shape(LATE, 2, levels, 8, H),
                shape(3 * levels, lat, dtype=BF16)]
        in_specs = [HBM] + [VM] * 5
        out_specs = [VM] * len(outs)
        scratch = [pltpu.SemaphoreType.DMA((2, blocks))]
    else:
        outs = [shape(levels, lon, lat), shape(2, 2, levels, 8, H), saved]
        in_specs = [VM] * 8
        out_specs = [HBM, VM, VM]
        scratch = [pltpu.VMEM((blocks, 2, levels, 8, H), F32), pltpu.VMEM((3 * levels, lat), BF16),
                   pltpu.SemaphoreType.DMA((2, blocks))]
    return pl.pallas_call(
        functools.partial(interior, first, EARLY, LATE, levels, lon),
        out_shape=outs,
        in_specs=in_specs,
        out_specs=out_specs,
        scratch_shapes=scratch + [ring, ring, ring, ring, ring, ring],
        compiler_params=params(LIM_A if first else LIM_B),
        name="interior",
    )(*operands)


def run_edges(levels, lon, lat, operands):
    window = lambda n: pltpu.VMEM((2, n, levels, lat), F32)
    return pl.pallas_call(
        functools.partial(edges, levels, lon),
        out_shape=shape(levels, lon, lat),
        in_specs=[VM] * 10 + [HBM],
        out_specs=HBM,
        input_output_aliases={10: 0},
        scratch_shapes=[
            pltpu.VMEM((2, 5, 24, lat), F32),
            window(8), window(8), window(8), window(10), window(8), window(8),
            pltpu.VMEM((2, 4, 3 * levels, lat), BF16),
            pltpu.VMEM((2, 2, levels, 8, H), F32),
            pltpu.VMEM((2, 4, levels + 8, lat), F32),
            pltpu.SemaphoreType.DMA((3, 2)),
        ],
        compiler_params=params(LIM_B),
        name="edges",
    )(*operands)


def shards(cotangent, synthesis, analysis, depths, metric, east_face, north_face):
    levels, lon, lat = cotangent.shape
    count = lax.axis_size("lon")
    parts = [metric, east_face, north_face, synthesis, analysis, depths[None]]
    total = 3 * lon + 2 * levels + 8
    small, at = 0.0, 0
    for part in parts:
        rows, width = part.shape
        small = small + jnp.pad(part, ((at, total - at - rows), (0, lat - width)))
        at += rows
    cols, ws, wa, co = run_prepare(levels, lon, lat, small)
    save_l, near, far, carried, blocks_in, blocks_out, z = run_interior(
        True, levels, lon, lat, (cotangent, small, cols, ws, wa, co))
    near = lax.ppermute(near, "lon", [(i, i ^ 1) for i in range(count)])
    far = lax.ppermute(far, "lon", [(i, (i + 2 * (i % 2) - 1) % count) for i in range(count)])
    out, edge_r, save_r = run_interior(
        False, levels, lon, lat, (cols, ws, wa, co, carried, blocks_in, blocks_out, z))
    return run_edges(levels, lon, lat, (near, far, small, cols, ws, wa, save_l, save_r, blocks_out, edge_r, out))


def solution(mesh):
    placed = (P(None, ("parts", "lon"), None), P(), P(), P(), P("lon", None), P("lon", None), P("lon", None))
    return jax.shard_map(
        shards, mesh=mesh, in_specs=placed, out_specs=P(None, ("parts", "lon"), None), check_vma=False)
```

```python
import functools
import math

import jax
import jax.numpy as jnp
from jax import lax
from jax.experimental import pallas as pl
from jax.experimental.pallas import tpu as pltpu
from jax.sharding import PartitionSpec as P

G = 16
H = 128
LIM_A, LIM_B = 28, 24
EARLY, LATE = 2, 3
COS1, COS2 = math.cos(2 * math.pi / 5), math.cos(4 * math.pi / 5)
SIN1, SIN2 = math.sin(2 * math.pi / 5) ** 2, math.sin(4 * math.pi / 5) ** 2


def column(row):
    n = row.shape[1]
    eye = lax.broadcasted_iota(jnp.int32, (n, n), 0) == lax.broadcasted_iota(jnp.int32, (n, n), 1)
    picked = jnp.sum(jnp.where(eye, jnp.broadcast_to(row, (n, n)), 0.0), axis=1, keepdims=True)
    return jnp.broadcast_to(picked, (n, H))


def split(x):
    high = x.astype(jnp.bfloat16)
    low = (x - high.astype(jnp.float32)).astype(jnp.bfloat16)
    return high, low


def prepare(lon, small, cols_ref, ws_ref, wa_ref, co):
    at = 3 * lon
    co[0, pl.ds(0, 8), :] = jnp.zeros((8, 2 * H), jnp.float32)
    fill_coefficients(co, 8, *(small[f * lon : (f + 1) * lon, :] for f in range(3)))
    n = ws_ref.shape[0]
    row = small[pl.ds(at + 2 * n, 1), :n]
    centre = 1.25 * row + 4.0
    half = 0.75 * row + 4.0
    product = row * (row + 4.0)
    c2, h2 = centre * centre, half * half
    gain = 16.0 / (centre * (16.0 * c2 * c2 - 20.0 * c2 * h2 + 5.0 * h2 * h2))
    d = column(row)
    cols_ref[0] = d
    cols_ref[1] = (1.0 - COS1) * (1.25 * d + 4.0)
    cols_ref[2] = (1.0 - COS2) * (1.25 * d + 4.0)
    cols_ref[3] = SIN1 * (d * (d + 4.0))
    cols_ref[4] = SIN2 * (d * (d + 4.0))
    for src, dst, scale in ((small[at : at + n, :n].T, ws_ref, None), (small[at + n : at + 2 * n, :n].T, wa_ref, gain)):
        if scale is not None:
            src = src * scale
        high, low = split(src)
        dst[:, :n] = high
        dst[:, n : 2 * n] = high
        dst[:, 2 * n :] = low


def mix(weights, field):
    high, low = split(field)
    stacked = jnp.concatenate([high, low, high], axis=0)
    return jnp.dot(weights, stacked, preferred_element_type=jnp.float32)


def halves(ref, slot, rows):
    return ref[slot, rows, :H], ref[slot, rows, H:]


def put(ref, slot, rows, pair):
    ref[slot, rows, :H] = pair[0]
    ref[slot, rows, H:] = pair[1]


def coefficients(co_ref, k):
    e = co_ref[0, pl.ds(k, 1), :]
    w = co_ref[0, pl.ds(k - 1, 1), :]
    n = co_ref[1, pl.ds(k, 1), :]
    s = co_ref[2, pl.ds(k, 1), :]
    return tuple((c[:, :H], c[:, H:]) for c in (e, w, n, s))


def operate(diag, y, east, west, co):
    lanes = lax.broadcasted_iota(jnp.int32, (G, H), 1)
    (ea, eb), (wa, wb), (na, nb), (sa, sb) = co
    ya, yb = y
    na_r, nb_r = pltpu.roll(ya, H - 1, 1), pltpu.roll(yb, H - 1, 1)
    sa_r, sb_r = pltpu.roll(ya, 1, 1), pltpu.roll(yb, 1, 1)
    na_r = jnp.where(lanes == H - 1, nb_r, na_r)
    sb_r = jnp.where(lanes == 0, sa_r, sb_r)
    a = (diag[0] * ya - ea * east[0]) - (wa * west[0] + na * na_r + sa * sa_r)
    b = (diag[1] * yb - eb * east[1]) - (wb * west[1] + nb * nb_r + sb * sb_r)
    return a, b


def fill_coefficients(co_ref, at, metric, east, north):
    rows = metric.shape[0]
    lanes = lax.broadcasted_iota(jnp.int32, (rows, H), 1)
    na, nb = north[:, :H], north[:, H:]
    sa, sb = pltpu.roll(na, 1, 1), pltpu.roll(nb, 1, 1)
    sb = jnp.where(lanes == 0, sa, sb)
    sa = jnp.where(lanes == 0, 0.0, sa)
    here = pl.ds(at, rows)
    co_ref[0, here, :] = east
    co_ref[1, here, :H] = na
    co_ref[1, here, H:] = jnp.where(lanes == H - 1, 0.0, nb)
    co_ref[2, here, :H] = sa
    co_ref[2, here, H:] = sb
    co_ref[3, here, :] = metric
    west = co_ref[0, pl.ds(at - 1, rows), :]
    faces = east + west + north
    co_ref[4, here, :H] = faces[:, :H] + sa
    co_ref[4, here, H:] = faces[:, H:] + sb


def diagonals(cols_ref, co_ref, k, rows):
    m, f = co_ref[3, pl.ds(k, 1), :], co_ref[4, pl.ds(k, 1), :]
    d, a1, a2 = cols_ref[0, rows, :], cols_ref[1, rows, :], cols_ref[2, rows, :]
    ta, tb = d * m[:, :H] + f[:, :H], d * m[:, H:] + f[:, H:]
    return (ta - a1, tb - a1), (ta - a2, tb - a2)


def add_scaled(pair, scale, old):
    return pair[0] + scale * old[0], pair[1] + scale * old[1]


def groups(levels):
    return [pl.ds(g * G, G) for g in range(levels // G)]


def step1(levels, cols, co, k, r, r_e, r_w, store, d1, d2):
    c = coefficients(co, k)
    for rows in groups(levels):
        first, second = diagonals(cols, co, k, rows)
        put(*d1, rows, first)
        put(*d2, rows, second)
        put(*store, rows, operate(first, halves(*r, rows), halves(*r_e, rows), halves(*r_w, rows), c))


def step_even(levels, cols, which, co, k, y, y_e, y_w, old, diag, store):
    c = coefficients(co, k)
    for rows in groups(levels):
        a, b = operate(halves(*diag, rows), halves(*y, rows), halves(*y_e, rows), halves(*y_w, rows), c)
        beta = cols[which, rows, :]
        oa, ob = halves(*old, rows)
        store(rows, (a + beta * oa, b + beta * ob))


def step3(levels, co, k, y, y_e, y_w, diag, store):
    c = coefficients(co, k)
    for rows in groups(levels):
        put(*store, rows, operate(halves(*diag, rows), halves(*y, rows), halves(*y_e, rows), halves(*y_w, rows), c))


def start(copies):
    for copy in copies:
        copy.start()


def wait(copies):
    for copy in copies:
        copy.wait()


def load_row(flat, block, j, levels):
    at = block * (2 * levels * 8) + j
    return jnp.concatenate([flat[pl.ds(at + h * levels * 8, levels, stride=8), :] for h in range(2)], axis=1)


def store_row(flat, block, j, levels, value):
    at = block * (2 * levels * 8) + j
    for h in range(2):
        flat[pl.ds(at + h * levels * 8, levels, stride=8), :] = value[:, h * H : (h + 1) * H]


RESUME = (("r", (2, 3, 0)), ("u", (1, 2)), ("y", (0, 1)), ("w", (3, 0)), ("d1", (2,)), ("d2", (0, 1, 2)))
CARRIED = sum(len(slots) for _, slots in RESUME)


def interior(first, early, late, levels, lon, *refs):
    refs = list(refs)
    take = lambda n: [refs.pop(0) for _ in range(n)]
    blocks = lon // 8
    begins = lax.axis_index("lon") < 2
    extra = begins & (lax.axis_index("parts") == 0)
    stop = jnp.where(begins, late, early)
    if first:
        x_ref, small, cols, ws, wa, co = take(6)
        save_ref, near, far, carried, cbuf, obuf, zbuf = take(7)
        (in_sem,) = take(1)
    else:
        cols, ws, wa, co, carried, cbuf, done, z_in = take(8)
        out_ref, edge_ref, save_ref = take(3)
        obuf, zbuf, out_sem = take(3)
    rr, uu, yy, ww, d1, d2 = take(6)
    assert not refs
    rings = {"r": rr, "u": uu, "y": yy, "w": ww, "d1": d1, "d2": d2}

    def fetch(b):
        return [
            pltpu.make_async_copy(x_ref.at[:, pl.ds(8 * b, 8), pl.ds(h * H, H)], cbuf.at[b, h], in_sem.at[h, b])
            for h in range(2)
        ]

    def flush(src, b):
        return [
            pltpu.make_async_copy(src.at[b, h], out_ref.at[:, pl.ds(8 * b, 8), pl.ds(h * H, H)], out_sem.at[h, b])
            for h in range(2)
        ]

    if first:
        for b in range(blocks):
            start(fetch(b))

    rows_in = cbuf.reshape(cbuf.shape[0] * 2 * levels * 8, H)
    rows_out = obuf.reshape(obuf.shape[0] * 2 * levels * 8, H)
    if first:
        wait(fetch(0))
        rr[0] = mix(ws[...], load_row(rows_in, 0, 0, levels))
        save_ref[0, 0] = rr[0]
    else:
        lax.fori_loop(1, stop - 1, lambda b, _: (start(flush(done, b)), 0)[1], 0)
        n = 0
        for name, slots in RESUME:
            for slot in slots:
                rings[name][slot] = carried[n]
                n += 1
        zbuf[...] = z_in[...]
        obuf[stop - 1] = done[stop - 1]

    def finish(row):
        o = jnp.dot(wa[...], zbuf[...], preferred_element_type=jnp.float32)
        store_row(rows_out, lax.div(row, 8), lax.rem(row, 8), levels, o)

    def store_z(rows, pair):
        start = rows.start
        for h in range(2):
            high, low = split(pair[h])
            lanes = slice(h * H, (h + 1) * H)
            zbuf[pl.ds(start, G), lanes] = high
            zbuf[pl.ds(levels + start, G), lanes] = low
            zbuf[pl.ds(2 * levels + start, G), lanes] = high

    def advance(t, s, stages):
        i = 8 * t + s
        k = 8 + i
        q = lambda n: (s + n) % 4
        if stages == 4:
            finish(i - 5)
        rr[(s + 1) % 4] = mix(ws[...], load_row(rows_in, t + (s + 1) // 8, (s + 1) % 8, levels))
        if not stages:
            return
        for rows in groups(levels):
            c1, c2, c3, c4 = (coefficients(co, k - min(n, stages)) for n in range(1, 5))
            at = lambda ref, n: halves(ref, q(n), rows)
            first_diag, second_diag = diagonals(cols, co, k - 1, rows)
            put(d1, q(3), rows, first_diag)
            put(d2, q(3), rows, second_diag)
            r = at(rr, 2)
            u = operate(first_diag, at(rr, 3), at(rr, 0), r, c1)
            put(uu, q(3), rows, u)
            if stages < 2:
                continue
            y = add_scaled(operate(at(d1, 2), at(uu, 2), u, at(uu, 1), c2), cols[3, rows, :], r)
            put(yy, q(2), rows, y)
            if stages < 3:
                continue
            old = at(yy, 0)
            w = operate(at(d2, 1), at(yy, 1), y, old, c3)
            put(ww, q(1), rows, w)
            if stages < 4:
                continue
            store_z(rows, add_scaled(operate(at(d2, 0), at(ww, 0), w, at(ww, 3), c4), cols[4, rows, :], old))

    def half(begin):
        if first:
            wait(fetch(stop + 1))
        for s in range(begin, begin + 4):
            advance(stop, s, 4)
        if not first:
            start(flush(obuf, stop - 1))

    def body(t, _):
        if first:

            @pl.when(t + 1 < blocks)
            def _():
                wait(fetch(t + 1))

        for s in range(8):
            advance(t, s, 4)

        if not first:

            @pl.when(t < blocks - 1)
            def _():
                start(flush(obuf, t - 1))

        return 0

    if first:
        wait(fetch(1))
        for s in range(8):
            advance(0, s, s // 2)
            if s == 3:
                save_ref[0, 1] = rr[1]
                save_ref[1, 0] = uu[1]
                save_ref[1, 1] = uu[2]
        save_ref[2, 0] = yy[2]
        save_ref[2, 1] = yy[3]
        save_ref[3, 0] = ww[3]
        save_ref[3, 1] = ww[0]
        lax.fori_loop(1, stop, body, 0)
        pl.when(extra)(functools.partial(half, 0))
        n = 0
        for name, slots in RESUME:
            for slot in slots:
                carried[n] = rings[name][slot]
                n += 1
        lax.fori_loop(jnp.where(extra, stop + 2, stop + 1), blocks, lambda b, _: (wait(fetch(b)), 0)[1], 0)
        even = lax.rem(lax.axis_index("lon"), 2) == 0
        for msg_ref, east in ((near, even), (far, jnp.logical_not(even))):
            block, row = jnp.where(east, blocks - 1, 0), jnp.where(east, 4, 0)
            at = jnp.where(east, lon - 4, 0)
            for j in range(4):
                msg_ref[j, :levels, :] = load_row(rows_in, block, row + j, levels)
                for f in range(3):
                    msg_ref[j, pl.ds(levels + f, 1), :] = small[pl.ds(f * lon + at + j, 1), :]
    else:
        pl.when(extra)(functools.partial(half, 4))
        lax.fori_loop(jnp.where(extra, stop + 1, stop), blocks, body, 0)
        finish(lon - 5)
        edge_ref[0] = obuf[blocks - 2]
        edge_ref[1] = obuf[blocks - 1]
        for f, (ref, row) in enumerate(((rr, lon - 2), (uu, lon - 3), (yy, lon - 4), (ww, lon - 5))):
            save_ref[f, 0] = ref[row % 4]
            save_ref[f, 1] = ref[(row + 1) % 4]
        lax.fori_loop(1, blocks - 2, lambda b, _: (wait(flush(obuf, b)), 0)[1], 0)


def edges(levels, lon, *refs):
    (near, far, small, cols, ws, wa, save_l, save_r, edge_l, edge_r, _out_in,
     out_ref, co, rr, uu, yy, ww, d1, d2, zbuf, obuf, halos, sems) = refs
    odd = lax.rem(lax.axis_index("lon"), 2)
    halos[1 - odd] = near[...]
    halos[odd] = far[...]
    copies = [
        pltpu.make_async_copy(edge_r.at[0, h], out_ref.at[:, pl.ds(lon - 16, 8), pl.ds(h * H, H)], sems.at[2, h])
        for h in range(2)
    ]
    start(copies)
    for side in range(2):
        halo = halos.at[side]
        c = co.at[side]
        c[0, pl.ds(0, 8), :] = jnp.zeros((8, 2 * H), jnp.float32)
        own = lon - 8 if side else 0
        mine = tuple(small[pl.ds(f * lon + own, 8), :] for f in range(3))
        theirs = [halo[:, levels + f, :] for f in range(3)]
        if side:
            window = [jnp.concatenate([a, b], axis=0) for a, b in zip(mine, theirs)]
            base = 8 + 4
        else:
            window = [jnp.concatenate([b, a], axis=0) for a, b in zip(mine, theirs)]
            base = 8
        fill_coefficients(c, 8, *window)
        r, u, y, w = rr.at[side], uu.at[side], yy.at[side], ww.at[side]
        e, g = d1.at[side], d2.at[side]
        save = save_r if side else save_l
        edge = edge_r.at[1] if side else edge_l.at[0]
        new_r = 4 if side else 0
        for j in range(4):
            r[new_r + j] = mix(ws[...], halo[j, :levels, :])
        u0, y0, w0, z0 = (3, 2, 1, 0) if side else (1, 2, 3, 4)
        old_r, old_u, old_y, old_w = (2, 1, 0, -1) if side else (4, 5, 6, 7)
        for f, (ref, row) in enumerate(((r, old_r), (u, old_u), (y, old_y), (w, old_w + 1))):
            ref[row] = save[f, 0]
            ref[row + 1] = save[f, 1]
        for n in range(0, 4) if side else range(4, 8):
            if not (u0 <= n < u0 + 4):
                for rows in groups(levels):
                    first, second = diagonals(cols, c, base + n, rows)
                    put(e, n, rows, first)
                    put(g, n, rows, second)
        for j in range(4):
            n = u0 + j
            step1(levels, cols, c, base + n, (r, n), (r, n + 1), (r, n - 1), (u, n), (e, n), (g, n))
        for j in range(4):
            n = y0 + j
            step_even(levels, cols, 3, c, base + n, (u, n), (u, n + 1), (u, n - 1), (r, n), (e, n),
                      lambda rows, pair, n=n: put(y, n, rows, pair))
        for j in range(4):
            n = w0 + j
            step3(levels, c, base + n, (y, n), (y, n + 1), (y, n - 1), (g, n), (w, n + 1))
        ob = obuf.at[side]
        ob[...] = edge[...]
        flat = ob.reshape(2 * levels * 8, H)
        for j in range(4):
            n = z0 + j
            z = zbuf.at[side, j]

            def store_z(rows, pair, z=z):
                start = rows.start
                for h in range(2):
                    high, low = split(pair[h])
                    lanes = slice(h * H, (h + 1) * H)
                    z[pl.ds(start, G), lanes] = high
                    z[pl.ds(levels + start, G), lanes] = low
                    z[pl.ds(2 * levels + start, G), lanes] = high

            step_even(levels, cols, 4, c, base + n, (w, n + 1), (w, n + 2), (w, n), (y, n), (g, n), store_z)
            o = jnp.dot(wa[...], z[...], preferred_element_type=jnp.float32)
            store_row(flat, 0, (4 + j) if side else j, levels, o)
        at = lon - 8 if side else 0
        for h in range(2):
            copies.append(pltpu.make_async_copy(ob.at[h], out_ref.at[:, pl.ds(at, 8), pl.ds(h * H, H)], sems.at[side, h]))
        start(copies[-2:])
    wait(copies)


F32, BF16 = jnp.float32, jnp.bfloat16
HBM = pl.BlockSpec(memory_space=pltpu.HBM)
ANY = pl.BlockSpec(memory_space=pl.ANY)
VM = pl.BlockSpec(memory_space=pltpu.VMEM)


def shape(*dims, dtype=F32):
    return jax.ShapeDtypeStruct(dims, dtype)


def params(mib):
    return pltpu.CompilerParams(vmem_limit_bytes=mib * 1024 * 1024)


def run_prepare(levels, lon, lat, small):
    mixer = shape(levels, 3 * levels, dtype=BF16)
    return pl.pallas_call(
        functools.partial(prepare, lon),
        out_shape=[shape(5, levels, H), mixer, mixer, shape(5, lon + 8, lat)],
        in_specs=[VM],
        out_specs=[VM] * 4,
        compiler_params=params(16),
        cost_estimate=pl.CostEstimate(flops=2 * 10**9, bytes_accessed=2**20, transcendentals=0),
        name="prepare",
    )(small)


def run_interior(first, levels, lon, lat, operands):
    ring = pltpu.VMEM((4, levels, lat), F32)
    blocks = lon // 8
    saved = shape(4, 2, levels, lat)
    if first:
        outs = [saved, shape(4, levels + 8, lat), shape(4, levels + 8, lat),
                shape(CARRIED, levels, lat), shape(blocks + 1, 2, levels, 8, H), shape(LATE + 1, 2, levels, 8, H),
                shape(3 * levels, lat, dtype=BF16)]
        in_specs = [HBM] + [VM] * 5
        out_specs = [VM] * len(outs)
        scratch = [pltpu.SemaphoreType.DMA((2, blocks))]
    else:
        outs = [shape(levels, lon, lat), shape(2, 2, levels, 8, H), saved]
        in_specs = [VM] * 8
        out_specs = [HBM, VM, VM]
        scratch = [pltpu.VMEM((blocks + 1, 2, levels, 8, H), F32), pltpu.VMEM((3 * levels, lat), BF16),
                   pltpu.SemaphoreType.DMA((2, blocks))]
    return pl.pallas_call(
        functools.partial(interior, first, EARLY, LATE, levels, lon),
        out_shape=outs,
        in_specs=in_specs,
        out_specs=out_specs,
        scratch_shapes=scratch + [ring, ring, ring, ring, ring, ring],
        compiler_params=params(LIM_A if first else LIM_B),
        name="interior",
    )(*operands)


def run_edges(levels, lon, lat, operands):
    window = lambda n: pltpu.VMEM((2, n, levels, lat), F32)
    return pl.pallas_call(
        functools.partial(edges, levels, lon),
        out_shape=shape(levels, lon, lat),
        in_specs=[VM] * 10 + [HBM],
        out_specs=HBM,
        input_output_aliases={10: 0},
        scratch_shapes=[
            pltpu.VMEM((2, 5, 24, lat), F32),
            window(8), window(8), window(8), window(10), window(8), window(8),
            pltpu.VMEM((2, 4, 3 * levels, lat), BF16),
            pltpu.VMEM((2, 2, levels, 8, H), F32),
            pltpu.VMEM((2, 4, levels + 8, lat), F32),
            pltpu.SemaphoreType.DMA((3, 2)),
        ],
        compiler_params=params(LIM_B),
        name="edges",
    )(*operands)


def shards(cotangent, synthesis, analysis, depths, metric, east_face, north_face):
    levels, lon, lat = cotangent.shape
    count = lax.axis_size("lon")
    parts = [metric, east_face, north_face, synthesis, analysis, depths[None]]
    total = 3 * lon + 2 * levels + 8
    small, at = 0.0, 0
    for part in parts:
        rows, width = part.shape
        small = small + jnp.pad(part, ((at, total - at - rows), (0, lat - width)))
        at += rows
    cols, ws, wa, co = run_prepare(levels, lon, lat, small)
    save_l, near, far, carried, blocks_in, blocks_out, z = run_interior(
        True, levels, lon, lat, (cotangent, small, cols, ws, wa, co))
    near = lax.ppermute(near, "lon", [(i, i ^ 1) for i in range(count)])
    far = lax.ppermute(far, "lon", [(i, (i + 2 * (i % 2) - 1) % count) for i in range(count)])
    out, edge_r, save_r = run_interior(
        False, levels, lon, lat, (cols, ws, wa, co, carried, blocks_in, blocks_out, z))
    return run_edges(levels, lon, lat, (near, far, small, cols, ws, wa, save_l, save_r, blocks_out, edge_r, out))


def solution(mesh):
    placed = (P(None, ("parts", "lon"), None), P(), P(), P(), P("lon", None), P("lon", None), P("lon", None))
    return jax.shard_map(
        shards, mesh=mesh, in_specs=placed, out_specs=P(None, ("parts", "lon"), None), check_vma=False)
```

```python
import functools
import math

import jax
import jax.numpy as jnp
from jax import lax
from jax.experimental import pallas as pl
from jax.experimental.pallas import tpu as pltpu
from jax.sharding import PartitionSpec as P

G = 16
H = 128
LIM_A, LIM_B = 28, 24
EARLY, LATE = 2, 3
COS1, COS2 = math.cos(2 * math.pi / 5), math.cos(4 * math.pi / 5)
SIN1, SIN2 = math.sin(2 * math.pi / 5) ** 2, math.sin(4 * math.pi / 5) ** 2


def column(row):
    n = row.shape[1]
    eye = lax.broadcasted_iota(jnp.int32, (n, n), 0) == lax.broadcasted_iota(jnp.int32, (n, n), 1)
    picked = jnp.sum(jnp.where(eye, jnp.broadcast_to(row, (n, n)), 0.0), axis=1, keepdims=True)
    return jnp.broadcast_to(picked, (n, H))


def split(x):
    high = x.astype(jnp.bfloat16)
    low = (x - high.astype(jnp.float32)).astype(jnp.bfloat16)
    return high, low


def prepare(lon, small, cols_ref, ws_ref, wa_ref, co):
    at = 3 * lon
    co[0, pl.ds(0, 8), :] = jnp.zeros((8, 2 * H), jnp.float32)
    fill_coefficients(co, 8, *(small[f * lon : (f + 1) * lon, :] for f in range(3)))
    n = ws_ref.shape[0]
    row = small[pl.ds(at + 2 * n, 1), :n]
    centre = 1.25 * row + 4.0
    half = 0.75 * row + 4.0
    product = row * (row + 4.0)
    c2, h2 = centre * centre, half * half
    gain = 16.0 / (centre * (16.0 * c2 * c2 - 20.0 * c2 * h2 + 5.0 * h2 * h2))
    d = column(row)
    cols_ref[0] = d
    cols_ref[1] = (1.0 - COS1) * (1.25 * d + 4.0)
    cols_ref[2] = (1.0 - COS2) * (1.25 * d + 4.0)
    cols_ref[3] = SIN1 * (d * (d + 4.0))
    cols_ref[4] = SIN2 * (d * (d + 4.0))
    for src, dst, scale in ((small[at : at + n, :n].T, ws_ref, None), (small[at + n : at + 2 * n, :n].T, wa_ref, gain)):
        if scale is not None:
            src = src * scale
        high, low = split(src)
        dst[:, :n] = high
        dst[:, n : 2 * n] = high
        dst[:, 2 * n :] = low


def mix(weights, field):
    high, low = split(field)
    stacked = jnp.concatenate([high, low, high], axis=0)
    return jnp.dot(weights, stacked, preferred_element_type=jnp.float32)


def halves(ref, slot, rows):
    return ref[slot, rows, :H], ref[slot, rows, H:]


def put(ref, slot, rows, pair):
    ref[slot, rows, :H] = pair[0]
    ref[slot, rows, H:] = pair[1]


def coefficients(co_ref, k):
    e = co_ref[0, pl.ds(k, 1), :]
    w = co_ref[0, pl.ds(k - 1, 1), :]
    n = co_ref[1, pl.ds(k, 1), :]
    s = co_ref[2, pl.ds(k, 1), :]
    return tuple((c[:, :H], c[:, H:]) for c in (e, w, n, s))


def operate(diag, y, east, west, co):
    lanes = lax.broadcasted_iota(jnp.int32, (G, H), 1)
    (ea, eb), (wa, wb), (na, nb), (sa, sb) = co
    ya, yb = y
    na_r, nb_r = pltpu.roll(ya, H - 1, 1), pltpu.roll(yb, H - 1, 1)
    sa_r, sb_r = pltpu.roll(ya, 1, 1), pltpu.roll(yb, 1, 1)
    na_r = jnp.where(lanes == H - 1, nb_r, na_r)
    sb_r = jnp.where(lanes == 0, sa_r, sb_r)
    a = (diag[0] * ya - ea * east[0]) - (wa * west[0] + na * na_r + sa * sa_r)
    b = (diag[1] * yb - eb * east[1]) - (wb * west[1] + nb * nb_r + sb * sb_r)
    return a, b


def fill_coefficients(co_ref, at, metric, east, north):
    rows = metric.shape[0]
    lanes = lax.broadcasted_iota(jnp.int32, (rows, H), 1)
    na, nb = north[:, :H], north[:, H:]
    sa, sb = pltpu.roll(na, 1, 1), pltpu.roll(nb, 1, 1)
    sb = jnp.where(lanes == 0, sa, sb)
    sa = jnp.where(lanes == 0, 0.0, sa)
    here = pl.ds(at, rows)
    co_ref[0, here, :] = east
    co_ref[1, here, :H] = na
    co_ref[1, here, H:] = jnp.where(lanes == H - 1, 0.0, nb)
    co_ref[2, here, :H] = sa
    co_ref[2, here, H:] = sb
    co_ref[3, here, :] = metric
    west = co_ref[0, pl.ds(at - 1, rows), :]
    faces = east + west + north
    co_ref[4, here, :H] = faces[:, :H] + sa
    co_ref[4, here, H:] = faces[:, H:] + sb


def diagonals(cols_ref, co_ref, k, rows):
    m, f = co_ref[3, pl.ds(k, 1), :], co_ref[4, pl.ds(k, 1), :]
    d, a1, a2 = cols_ref[0, rows, :], cols_ref[1, rows, :], cols_ref[2, rows, :]
    ta, tb = d * m[:, :H] + f[:, :H], d * m[:, H:] + f[:, H:]
    return (ta - a1, tb - a1), (ta - a2, tb - a2)


def add_scaled(pair, scale, old):
    return pair[0] + scale * old[0], pair[1] + scale * old[1]


def groups(levels):
    return [pl.ds(g * G, G) for g in range(levels // G)]


def step1(levels, cols, co, k, r, r_e, r_w, store, d1, d2):
    c = coefficients(co, k)
    for rows in groups(levels):
        first, second = diagonals(cols, co, k, rows)
        put(*d1, rows, first)
        put(*d2, rows, second)
        put(*store, rows, operate(first, halves(*r, rows), halves(*r_e, rows), halves(*r_w, rows), c))


def step_even(levels, cols, which, co, k, y, y_e, y_w, old, diag, store):
    c = coefficients(co, k)
    for rows in groups(levels):
        a, b = operate(halves(*diag, rows), halves(*y, rows), halves(*y_e, rows), halves(*y_w, rows), c)
        beta = cols[which, rows, :]
        oa, ob = halves(*old, rows)
        store(rows, (a + beta * oa, b + beta * ob))


def step3(levels, co, k, y, y_e, y_w, diag, store):
    c = coefficients(co, k)
    for rows in groups(levels):
        put(*store, rows, operate(halves(*diag, rows), halves(*y, rows), halves(*y_e, rows), halves(*y_w, rows), c))


def start(copies):
    for copy in copies:
        copy.start()


def wait(copies):
    for copy in copies:
        copy.wait()


def load_row(flat, block, j, levels):
    at = block * (2 * levels * 8) + j
    return jnp.concatenate([flat[pl.ds(at + h * levels * 8, levels, stride=8), :] for h in range(2)], axis=1)


def store_row(flat, block, j, levels, value):
    at = block * (2 * levels * 8) + j
    for h in range(2):
        flat[pl.ds(at + h * levels * 8, levels, stride=8), :] = value[:, h * H : (h + 1) * H]


RESUME = (("r", (2, 3, 0)), ("u", (1, 2)), ("y", (0, 1)), ("w", (3, 0)), ("d1", (2,)), ("d2", (0, 1, 2)))
CARRIED = sum(len(slots) for _, slots in RESUME)


def interior(first, early, late, levels, lon, *refs):
    refs = list(refs)
    take = lambda n: [refs.pop(0) for _ in range(n)]
    blocks = lon // 8
    begins = lax.axis_index("lon") < 2
    extra = begins & (lax.axis_index("parts") == 0)
    stop = jnp.where(begins, late, early)
    if first:
        x_ref, small, cols, ws, wa, co = take(6)
        save_ref, near, far, carried, obuf, zbuf = take(6)
    else:
        x_ref, cols, ws, wa, co, carried, done, z_in = take(8)
        out_ref, edge_ref, save_ref = take(3)
        obuf, zbuf, out_sem = take(3)
    cbuf, rr, uu, yy, ww, d1, d2 = take(7)
    assert not refs
    rings = {"r": rr, "u": uu, "y": yy, "w": ww, "d1": d1, "d2": d2}

    def bring(b):
        for h in range(2):
            cbuf[0, h] = x_ref[:, b, h]

    def flush(src, b):
        return [
            pltpu.make_async_copy(src.at[b, h], out_ref.at[:, pl.ds(8 * b, 8), pl.ds(h * H, H)], out_sem.at[h, b])
            for h in range(2)
        ]

    bring(0 if first else stop)
    rows_in = cbuf.reshape(cbuf.shape[0] * 2 * levels * 8, H)
    rows_out = obuf.reshape(obuf.shape[0] * 2 * levels * 8, H)
    if first:
        rr[0] = mix(ws[...], load_row(rows_in, 0, 0, levels))
        save_ref[0, 0] = rr[0]
    else:
        lax.fori_loop(1, stop - 1, lambda b, _: (start(flush(done, b)), 0)[1], 0)
        n = 0
        for name, slots in RESUME:
            for slot in slots:
                rings[name][slot] = carried[n]
                n += 1
        zbuf[...] = z_in[...]
        obuf[stop - 1] = done[stop - 1]

    def finish(row):
        o = jnp.dot(wa[...], zbuf[...], preferred_element_type=jnp.float32)
        store_row(rows_out, lax.div(row, 8), lax.rem(row, 8), levels, o)

    def store_z(rows, pair):
        start = rows.start
        for h in range(2):
            high, low = split(pair[h])
            lanes = slice(h * H, (h + 1) * H)
            zbuf[pl.ds(start, G), lanes] = high
            zbuf[pl.ds(levels + start, G), lanes] = low
            zbuf[pl.ds(2 * levels + start, G), lanes] = high

    def advance(t, s, stages):
        i = 8 * t + s
        k = 8 + i
        q = lambda n: (s + n) % 4
        if stages == 4:
            finish(i - 5)
        if s == 7:
            bring(jnp.minimum(t + 1, blocks - 1))
        rr[(s + 1) % 4] = mix(ws[...], load_row(rows_in, 0, (s + 1) % 8, levels))
        if not stages:
            return
        for rows in groups(levels):
            c1, c2, c3, c4 = (coefficients(co, k - min(n, stages)) for n in range(1, 5))
            at = lambda ref, n: halves(ref, q(n), rows)
            first_diag, second_diag = diagonals(cols, co, k - 1, rows)
            put(d1, q(3), rows, first_diag)
            put(d2, q(3), rows, second_diag)
            r = at(rr, 2)
            u = operate(first_diag, at(rr, 3), at(rr, 0), r, c1)
            put(uu, q(3), rows, u)
            if stages < 2:
                continue
            y = add_scaled(operate(at(d1, 2), at(uu, 2), u, at(uu, 1), c2), cols[3, rows, :], r)
            put(yy, q(2), rows, y)
            if stages < 3:
                continue
            old = at(yy, 0)
            w = operate(at(d2, 1), at(yy, 1), y, old, c3)
            put(ww, q(1), rows, w)
            if stages < 4:
                continue
            store_z(rows, add_scaled(operate(at(d2, 0), at(ww, 0), w, at(ww, 3), c4), cols[4, rows, :], old))

    def half(begin):
        for s in range(begin, begin + 4):
            advance(stop, s, 4)
        if not first:
            start(flush(obuf, stop - 1))

    def body(t, _):
        for s in range(8):
            advance(t, s, 4)

        if not first:

            @pl.when(t < blocks - 1)
            def _():
                start(flush(obuf, t - 1))

        return 0

    if first:
        for s in range(8):
            advance(0, s, s // 2)
            if s == 3:
                save_ref[0, 1] = rr[1]
                save_ref[1, 0] = uu[1]
                save_ref[1, 1] = uu[2]
        save_ref[2, 0] = yy[2]
        save_ref[2, 1] = yy[3]
        save_ref[3, 0] = ww[3]
        save_ref[3, 1] = ww[0]
        lax.fori_loop(1, stop, body, 0)
        pl.when(extra)(functools.partial(half, 0))
        n = 0
        for name, slots in RESUME:
            for slot in slots:
                carried[n] = rings[name][slot]
                n += 1
        even = lax.rem(lax.axis_index("lon"), 2) == 0
        for msg_ref, east in ((near, even), (far, jnp.logical_not(even))):
            block, row = jnp.where(east, blocks - 1, 0), jnp.where(east, 4, 0)
            at = jnp.where(east, lon - 4, 0)
            bring(block)
            for j in range(4):
                msg_ref[j, :levels, :] = load_row(rows_in, 0, row + j, levels)
                for f in range(3):
                    msg_ref[j, pl.ds(levels + f, 1), :] = small[pl.ds(f * lon + at + j, 1), :]
    else:
        pl.when(extra)(functools.partial(half, 4))
        lax.fori_loop(jnp.where(extra, stop + 1, stop), blocks, body, 0)
        finish(lon - 5)
        edge_ref[0] = obuf[blocks - 2]
        edge_ref[1] = obuf[blocks - 1]
        for f, (ref, row) in enumerate(((rr, lon - 2), (uu, lon - 3), (yy, lon - 4), (ww, lon - 5))):
            save_ref[f, 0] = ref[row % 4]
            save_ref[f, 1] = ref[(row + 1) % 4]
        lax.fori_loop(1, blocks - 2, lambda b, _: (wait(flush(obuf, b)), 0)[1], 0)


def edges(levels, lon, *refs):
    (near, far, small, cols, ws, wa, save_l, save_r, edge_l, edge_r, _out_in,
     out_ref, co, rr, uu, yy, ww, d1, d2, zbuf, obuf, halos, sems) = refs
    odd = lax.rem(lax.axis_index("lon"), 2)
    halos[1 - odd] = near[...]
    halos[odd] = far[...]
    copies = [
        pltpu.make_async_copy(edge_r.at[0, h], out_ref.at[:, pl.ds(lon - 16, 8), pl.ds(h * H, H)], sems.at[2, h])
        for h in range(2)
    ]
    start(copies)
    for side in range(2):
        halo = halos.at[side]
        c = co.at[side]
        c[0, pl.ds(0, 8), :] = jnp.zeros((8, 2 * H), jnp.float32)
        own = lon - 8 if side else 0
        mine = tuple(small[pl.ds(f * lon + own, 8), :] for f in range(3))
        theirs = [halo[:, levels + f, :] for f in range(3)]
        if side:
            window = [jnp.concatenate([a, b], axis=0) for a, b in zip(mine, theirs)]
            base = 8 + 4
        else:
            window = [jnp.concatenate([b, a], axis=0) for a, b in zip(mine, theirs)]
            base = 8
        fill_coefficients(c, 8, *window)
        r, u, y, w = rr.at[side], uu.at[side], yy.at[side], ww.at[side]
        e, g = d1.at[side], d2.at[side]
        save = save_r if side else save_l
        edge = edge_r.at[1] if side else edge_l.at[0]
        new_r = 4 if side else 0
        for j in range(4):
            r[new_r + j] = mix(ws[...], halo[j, :levels, :])
        u0, y0, w0, z0 = (3, 2, 1, 0) if side else (1, 2, 3, 4)
        old_r, old_u, old_y, old_w = (2, 1, 0, -1) if side else (4, 5, 6, 7)
        for f, (ref, row) in enumerate(((r, old_r), (u, old_u), (y, old_y), (w, old_w + 1))):
            ref[row] = save[f, 0]
            ref[row + 1] = save[f, 1]
        for n in range(0, 4) if side else range(4, 8):
            if not (u0 <= n < u0 + 4):
                for rows in groups(levels):
                    first, second = diagonals(cols, c, base + n, rows)
                    put(e, n, rows, first)
                    put(g, n, rows, second)
        for j in range(4):
            n = u0 + j
            step1(levels, cols, c, base + n, (r, n), (r, n + 1), (r, n - 1), (u, n), (e, n), (g, n))
        for j in range(4):
            n = y0 + j
            step_even(levels, cols, 3, c, base + n, (u, n), (u, n + 1), (u, n - 1), (r, n), (e, n),
                      lambda rows, pair, n=n: put(y, n, rows, pair))
        for j in range(4):
            n = w0 + j
            step3(levels, c, base + n, (y, n), (y, n + 1), (y, n - 1), (g, n), (w, n + 1))
        ob = obuf.at[side]
        for h in range(2):
            ob[h] = edge[h]
        flat = ob.reshape(3 * levels * 8, H)
        for j in range(4):
            n = z0 + j
            z = zbuf.at[side, j]

            def store_z(rows, pair, z=z):
                start = rows.start
                for h in range(2):
                    high, low = split(pair[h])
                    lanes = slice(h * H, (h + 1) * H)
                    z[pl.ds(start, G), lanes] = high
                    z[pl.ds(levels + start, G), lanes] = low
                    z[pl.ds(2 * levels + start, G), lanes] = high

            step_even(levels, cols, 4, c, base + n, (w, n + 1), (w, n + 2), (w, n), (y, n), (g, n), store_z)
            o = jnp.dot(wa[...], z[...], preferred_element_type=jnp.float32)
            store_row(flat, 0, (4 + j) if side else j, levels, o)
        at = lon - 8 if side else 0
        for h in range(2):
            copies.append(pltpu.make_async_copy(ob.at[h], out_ref.at[:, pl.ds(at, 8), pl.ds(h * H, H)], sems.at[side, h]))
        start(copies[-2:])
    wait(copies)


F32, BF16 = jnp.float32, jnp.bfloat16
HBM = pl.BlockSpec(memory_space=pltpu.HBM)
ANY = pl.BlockSpec(memory_space=pl.ANY)
VM = pl.BlockSpec(memory_space=pltpu.VMEM)


def shape(*dims, dtype=F32):
    return jax.ShapeDtypeStruct(dims, dtype)


def params(mib):
    return pltpu.CompilerParams(vmem_limit_bytes=mib * 1024 * 1024)


def run_prepare(levels, lon, lat, small):
    mixer = shape(levels, 3 * levels, dtype=BF16)
    return pl.pallas_call(
        functools.partial(prepare, lon),
        out_shape=[shape(5, levels, H), mixer, mixer, shape(5, lon + 8, lat)],
        in_specs=[VM],
        out_specs=[VM] * 4,
        compiler_params=params(16),
        cost_estimate=pl.CostEstimate(flops=2 * 10**9, bytes_accessed=2**20, transcendentals=0),
        name="prepare",
    )(small)


def run_interior(first, levels, lon, lat, operands):
    ring = pltpu.VMEM((4, levels, lat), F32)
    blocks = lon // 8
    saved = shape(4, 2, levels, lat)
    if first:
        outs = [saved, shape(4, levels + 8, lat), shape(4, levels + 8, lat),
                shape(CARRIED, levels, lat), shape(LATE + 1, 2, levels, 8, H),
                shape(3 * levels, lat, dtype=BF16)]
        in_specs = [VM] * 6
        out_specs = [VM] * len(outs)
        scratch = []
    else:
        outs = [shape(levels, lon, lat), shape(2, 2, levels, 8, H), saved]
        in_specs = [VM] * 8
        out_specs = [HBM, VM, VM]
        scratch = [pltpu.VMEM((blocks + 1, 2, levels, 8, H), F32), pltpu.VMEM((3 * levels, lat), BF16),
                   pltpu.SemaphoreType.DMA((2, blocks))]
    return pl.pallas_call(
        functools.partial(interior, first, EARLY, LATE, levels, lon),
        out_shape=outs,
        in_specs=in_specs,
        out_specs=out_specs,
        scratch_shapes=scratch + [pltpu.VMEM((2, 2, levels, 8, H), F32), ring, ring, ring, ring, ring, ring],
        compiler_params=params(LIM_A if first else LIM_B),
        name="interior",
    )(*operands)


def run_edges(levels, lon, lat, operands):
    window = lambda n: pltpu.VMEM((2, n, levels, lat), F32)
    return pl.pallas_call(
        functools.partial(edges, levels, lon),
        out_shape=shape(levels, lon, lat),
        in_specs=[VM] * 10 + [HBM],
        out_specs=HBM,
        input_output_aliases={10: 0},
        scratch_shapes=[
            pltpu.VMEM((2, 5, 24, lat), F32),
            window(8), window(8), window(8), window(10), window(8), window(8),
            pltpu.VMEM((2, 4, 3 * levels, lat), BF16),
            pltpu.VMEM((2, 3, levels, 8, H), F32),
            pltpu.VMEM((2, 4, levels + 8, lat), F32),
            pltpu.SemaphoreType.DMA((3, 2)),
        ],
        compiler_params=params(LIM_B),
        name="edges",
    )(*operands)


def shards(cotangent, synthesis, analysis, depths, metric, east_face, north_face):
    levels, lon, lat = cotangent.shape
    count = lax.axis_size("lon")
    parts = [metric, east_face, north_face, synthesis, analysis, depths[None]]
    total = 3 * lon + 2 * levels + 8
    small, at = 0.0, 0
    for part in parts:
        rows, width = part.shape
        small = small + jnp.pad(part, ((at, total - at - rows), (0, lat - width)))
        at += rows
    cols, ws, wa, co = run_prepare(levels, lon, lat, small)
    tiles = cotangent.reshape(levels, lon // 8, 8, 2, H).transpose(0, 1, 3, 2, 4)
    save_l, near, far, carried, blocks_out, z = run_interior(
        True, levels, lon, lat, (tiles, small, cols, ws, wa, co))
    near = lax.ppermute(near, "lon", [(i, i ^ 1) for i in range(count)])
    far = lax.ppermute(far, "lon", [(i, (i + 2 * (i % 2) - 1) % count) for i in range(count)])
    out, edge_r, save_r = run_interior(
        False, levels, lon, lat, (tiles, cols, ws, wa, co, carried, blocks_out, z))
    return run_edges(levels, lon, lat, (near, far, small, cols, ws, wa, save_l, save_r, blocks_out, edge_r, out))


def solution(mesh):
    placed = (P(None, ("parts", "lon"), None), P(), P(), P(), P("lon", None), P("lon", None), P("lon", None))
    return jax.shard_map(
        shards, mesh=mesh, in_specs=placed, out_specs=P(None, ("parts", "lon"), None), check_vma=False)
```
